32 devices in a mesh: groups: 2 (over x), dp: 16 (over z, y, core).
Axes of the slice: x: 2, y: 2, z: 4, core: 2. Of those that a mesh axis runs over, the one named last changes fastest.
Arguments:
- x_rows: bfloat16 [8192, 5120], P(('groups', 'dp')), parts along dimension 0, may hold values from -6 to 6
- query_rows: bfloat16 [8192, 4096], P(('groups', 'dp')), parts along dimension 0, may hold values from -160 to 160
- key_rows: bfloat16 [8192, 512], P(('groups', 'dp')), parts along dimension 0, may hold values from -6 to 6
- values_base: bfloat16 [8192, 512], P(('groups', 'dp')), parts along dimension 0, may hold values from -6 to 6
- grad_out: bfloat16 [8192, 4096], P(('groups', 'dp')), parts along dimension 0, may hold values from -6 to 6
- adapt_down: bfloat16 [16, 64, 5120], P('dp'), may hold values from -0.078125 to 0.078125
- adapt_up: bfloat16 [16, 64, 512], P('dp'), may hold values from -0.75 to 0.75
- block_tenant: int32 [64], P(('groups', 'dp')), parts along dimension 0, may hold values from 0 to 15
- owner_map: int32 [16], replicated, may hold values from 0 to 15, each once
- seq_ids: int32 [64, 128], P(('groups', 'dp')), parts along dimension 0, may hold values from 0 to 3, never falling along the last dimension, each value on 1 to 64 neighbouring positions
Outputs:
- grad_query: bfloat16 [8192, 4096], P(('groups', 'dp')), parts along dimension 0
- grad_input_t: bfloat16 [5120, 8192], P('dp', 'groups'), parts along dimension 1
- grad_down: bfloat16 [32, 64, 5120], P(('groups', 'dp')), parts along dimension 0
- grad_up: bfloat16 [32, 64, 512], P(('groups', 'dp')), parts along dimension 0
The draws below stay inside these ranges and needn't reach their ends.
There are 2 independent parts, one for each index of `groups`. The reference program is written for one: setup_inputs(seed, part) draws one part's arguments, and reference() takes and returns one part's arrays. A program takes and returns all parts, laid end to end along the dimension named above; an argument that names none is the same for every part. Nothing has to cross between parts.
All inputs are finite; a program needn't handle non-finite values.
Results may differ from the reference program's by a relative error of at most 0.0071.
Values may be sent and summed in bfloat16 or wider, within the bound.
No kernel may reach another device: no remote copies, remote signals or barrier semaphores. Data moves between devices by JAX's collectives and lax.ppermute only.
A program may use at most 128 MiB of HBM per device.

```python
import math
import jax
import jax.numpy as jnp
import numpy as np
from jax import lax

D = 5120
HD = 128
KVH = 4
R = 64
BLOCK = 128
SEGS = 4
MOST = 64
GROUP = 8
QW = 4096
KW = 512
BLOCKS = 32
TOKENS = 4096
ADAPTERS = 16


def shared_keys(key):
    return jnp.clip(jax.random.normal(key, (TOKENS, KW), jnp.float32), -6.0, 6.0)


def draw_key_rows(key, part):
    base_keys = shared_keys(key)
    return base_keys.astype(jnp.bfloat16)


def draw_query_rows(key, part):
    key = jax.random.fold_in(key, 5)
    first_key = jax.random.fold_in(key, 0)
    drawn_query = jnp.clip(jax.random.normal(first_key, (TOKENS, QW), jnp.float32), -6.0, 6.0)
    return drawn_query.astype(jnp.bfloat16)


def touch_ends(drawn, key, smallest, high):
    longest = drawn.shape.index(max(drawn.shape))
    spots = []
    for shift in (0, 1):
        where = [jax.random.randint(jax.random.fold_in(key, axis), (), 0, length) for axis, length in enumerate(drawn.shape)]
        where[longest] = (where[longest] + shift) % drawn.shape[longest]
        spots.append(tuple(where))
    return drawn.at[spots[0]].set(smallest).at[spots[1]].set(high)


def block_scale(stream_key, dims, cuts, low, high):
    def one(dim, shards_of):
        steps = jax.random.uniform(jax.random.fold_in(jax.random.fold_in(stream_key, 6), dim), (shards_of,), jnp.float32, low / len(cuts), high / len(cuts))
        return jnp.repeat(jnp.exp(steps), dims[dim] // shards_of).reshape((-1,) + (1,) * (len(dims) - dim - 1))

    level = one(*cuts[0])
    for cut in cuts[1:]:
        level = level * one(*cut)
    return level


def rank_bounds(count, lean):
    weights = [(1 << 20) // math.isqrt(grade ** lean) + 1 for grade in range(1, count + 1)]
    scale = 1 + sum(weights) // (1 << 30)
    return np.cumsum(np.array([max(1, weight // scale) for weight in weights]))


def skewed_ids(stream_key, dims, count, lean):
    grid = rank_bounds(count, lean)
    ticket = jax.random.randint(jax.random.fold_in(stream_key, 1), dims, 0, int(grid[count - 1]))
    standing = jnp.searchsorted(jnp.asarray(grid, jnp.int32), ticket, side="right")
    return jax.random.permutation(jax.random.fold_in(stream_key, 2), count)[standing].astype(jnp.int32)


def split_up(number_of, total, reach, skew):
    loads = [(1 << 20) // math.isqrt(grade ** skew) + 1 for grade in range(2, number_of + 1)]
    spare, given = total - reach - (number_of - 1), [1] * (number_of - 1)
    while spare > 0:
        movable = [i for i in range(number_of - 1) if given[i] < reach]
        whole, budget = sum([loads[i] for i in movable]), spare
        for i in movable:
            more = min(reach - given[i], max(1, budget * loads[i] // whole), spare)
            given[i] = given[i] + more
            spare = spare - more
    return np.array([reach] + given)


def ragged(own_key, number_of, total, reach, lean):
    if number_of == 2:
        one = jax.random.randint(own_key, (), max(1, total - reach), min(reach, total - 1) + 1)
        return jnp.stack([one, total - one])
    tallies = jnp.asarray(split_up(number_of, total, reach, lean), jnp.int32)
    twos = (number_of - 1) // 2
    source_of, taker = tallies[1:1 + 2 * twos:2], tallies[2:2 + 2 * twos:2]
    margin = jnp.minimum(source_of - 1, reach - taker)
    moved = jax.random.randint(jax.random.fold_in(own_key, 1), (twos,), 0, 1 << 20) % (margin + 1)
    tallies = tallies.at[1:1 + 2 * twos:2].set(source_of - moved).at[2:2 + 2 * twos:2].set(taker + moved)
    return tallies[jax.random.permutation(jax.random.fold_in(own_key, 2), number_of)]


def noise(own_key, extent, scale, most, pieces=(), kind=jnp.bfloat16):
    drawn = jax.random.normal(own_key, extent, jnp.float32) * scale
    if len(pieces) > 0:
        drawn = block_scale(own_key, extent, pieces, -0.22, 0.18) * drawn
    return jnp.clip(drawn, min=-most, max=most).astype(kind)


def setup_inputs(seed: int = 0, part: int = 0) -> dict:
    streams_of = jax.random.split(jax.random.key(seed), 11)
    own_keys = jax.random.split(jax.random.fold_in(streams_of[10], part), 11)
    return {
        "x_rows": noise(own_keys[0], (TOKENS, D), 1.0, 6.0, ((0, 16),)),
        "query_rows": draw_query_rows(jax.random.fold_in(jax.random.fold_in(streams_of[10], part), 71), part),
        "key_rows": draw_key_rows(jax.random.fold_in(jax.random.fold_in(streams_of[10], part), 71), part),
        "values_base": noise(own_keys[3], (TOKENS, KW), 1.0, 6.0, ((0, 16),)),
        "grad_out": noise(own_keys[4], (TOKENS, QW), 1.0, 6.0, ((0, 16),)),
        "adapt_down": noise(streams_of[5], (ADAPTERS, R, D), D ** -0.5, 0.078125, ((0, 16),)),
        "adapt_up": noise(streams_of[6], (ADAPTERS, R, KW), R ** -0.5, 0.75, ((0, 16),)),
        "block_tenant": touch_ends(skewed_ids(own_keys[7], (BLOCKS,), ADAPTERS, 2), jax.random.fold_in(own_keys[7], 3), 0, ADAPTERS - 1).astype(jnp.int32),
        "owner_map": jax.random.permutation(streams_of[8], ADAPTERS).astype(jnp.int32),
        "seq_ids": jax.vmap(lambda own: jnp.searchsorted(jnp.cumsum(ragged(own, SEGS, BLOCK, MOST, 0)), jnp.arange(BLOCK), side="right"))(jax.random.split(own_keys[9], BLOCKS)).reshape((BLOCKS, BLOCK)).astype(jnp.int32),
    }


adapter_scale = 2.0
neg_fill = -1e+30

def build_mask(seg_ids, block_len):
    position = jnp.arange(seg_ids.shape[0])
    block_ids = position // block_len
    same_block = block_ids[:, None] == block_ids[None, :]
    same_seq = seg_ids[:, None] == seg_ids[None, :]
    causal = position[None, :] <= position[:, None]
    return same_block & same_seq & causal

def first_pass(query_tile, key_tile, grad_tile, keep_mask):
    tile_rows = query_tile.shape[0]
    query_heads = query_tile.reshape(tile_rows, KVH, GROUP, HD).astype(jnp.float32)
    key_heads = key_tile.reshape(tile_rows, KVH, HD).astype(jnp.float32)
    scores = jnp.einsum('tkgd,skd->kgts', query_heads, key_heads) / math.sqrt(HD)
    scores = jnp.where(keep_mask[None, None], scores, neg_fill)
    attn_probs = jax.nn.softmax(scores, axis=-1)
    probs_b = attn_probs.astype(jnp.bfloat16)
    grad_heads = grad_tile.reshape(tile_rows, KVH, GROUP, HD).astype(jnp.float32)
    value_gradient = jnp.einsum('kgts,tkgd->skd', probs_b.astype(jnp.float32), grad_heads)
    return (attn_probs, probs_b, value_gradient.reshape(tile_rows, KVH * HD).astype(jnp.bfloat16))

def second_pass(attn_probs, probs_b, value_tile, key_tile, grad_tile):
    tile_rows = value_tile.shape[0]
    value_heads = value_tile.reshape(tile_rows, KVH, HD).astype(jnp.float32)
    key_heads = key_tile.reshape(tile_rows, KVH, HD).astype(jnp.float32)
    grad_heads = grad_tile.reshape(tile_rows, KVH, GROUP, HD).astype(jnp.float32)
    out_attn = jnp.einsum('kgts,skd->tkgd', probs_b.astype(jnp.float32), value_heads)
    dprobs = jnp.einsum('tkgd,skd->kgts', grad_heads, value_heads)
    row_delta = jnp.transpose(lax.optimization_barrier(jnp.sum(grad_heads * out_attn, axis=-1)), (1, 2, 0))[..., None]
    dscores = (attn_probs * (dprobs - row_delta)).astype(jnp.bfloat16)
    grad_heads_q = jnp.einsum('kgts,skd->tkgd', dscores.astype(jnp.float32), key_heads) / math.sqrt(HD)
    return grad_heads_q.reshape(tile_rows, KVH * GROUP * HD).astype(jnp.bfloat16)

def reference(x_rows, query_rows, key_rows, values_base, grad_out, adapt_down, adapt_up, block_tenant, owner_map, seq_ids):
    store_rows = owner_map[block_tenant].astype(jnp.int32)
    items = (x_rows.reshape(BLOCKS, BLOCK, D), query_rows.reshape(BLOCKS, BLOCK, QW), key_rows.reshape(BLOCKS, BLOCK, KW), values_base.reshape(BLOCKS, BLOCK, KW), grad_out.reshape(BLOCKS, BLOCK, QW), seq_ids, store_rows)

    def step(carry, item):
        sum_down, sum_up = carry
        x_block, q_block, k_block, value_block, g_block, seg_block, store_row = item
        down_factor = lax.dynamic_index_in_dim(adapt_down, store_row, 0, keepdims=False)
        up_weight_matrix = lax.dynamic_index_in_dim(adapt_up, store_row, 0, keepdims=False)
        keep_mask = build_mask(seg_block, BLOCK)
        attn_probs, probs_b, value_gradient = first_pass(q_block, k_block, g_block, keep_mask)
        hidden_rows = jnp.dot(x_block, down_factor.T, preferred_element_type=jnp.float32).astype(jnp.bfloat16)
        value_rows = (value_block.astype(jnp.float32) + adapter_scale * jnp.dot(hidden_rows, up_weight_matrix, preferred_element_type=jnp.float32)).astype(jnp.bfloat16)
        hidden_gradient = (adapter_scale * jnp.dot(value_gradient, up_weight_matrix.T, preferred_element_type=jnp.float32)).astype(jnp.bfloat16)
        part_down = jnp.dot(hidden_gradient.T, x_block, preferred_element_type=jnp.float32)
        partial_up_weight = adapter_scale * jnp.dot(hidden_rows.T, value_gradient, preferred_element_type=jnp.float32)
        sum_down = sum_down.at[store_row].add(part_down)
        sum_up = sum_up.at[store_row].add(partial_up_weight)
        grad_q = second_pass(attn_probs, probs_b, value_rows, k_block, g_block)
        grad_x = jnp.dot(hidden_gradient, down_factor, preferred_element_type=jnp.float32).astype(jnp.bfloat16)
        return ((sum_down, sum_up), (grad_q, grad_x))
    start = (jnp.zeros((ADAPTERS, R, D), jnp.float32), jnp.zeros((ADAPTERS, R, KW), jnp.float32))
    (sum_down, sum_up), (grad_q, grad_x) = lax.scan(step, start, items)
    grad_query = grad_q.reshape(TOKENS, QW)
    grad_input_t = grad_x.reshape(TOKENS, D).T
    return (grad_query, grad_input_t, sum_down.astype(jnp.bfloat16), sum_up.astype(jnp.bfloat16))
```

```python
import math

import jax
import jax.numpy as jnp
from jax import lax
from jax.experimental import pallas as pl
from jax.experimental.pallas import tpu as pltpu
from jax.sharding import PartitionSpec as P

HD = 128
KVH = 4
GROUP = 8
CLUSTER = 8
SPAN = 16


adapter_scale = 2.0
neg_fill = -1e30


def build_mask(seg_ids, block_len):
    position = jnp.arange(seg_ids.shape[0])
    block_ids = position // block_len
    same_block = block_ids[:, None] == block_ids[None, :]
    same_seq = seg_ids[:, None] == seg_ids[None, :]
    causal = position[None, :] <= position[:, None]
    return same_block & same_seq & causal


def first_pass(query_tile, key_tile, grad_tile, keep_mask):
    tile_rows = query_tile.shape[0]
    query_heads = query_tile.reshape(tile_rows, KVH, GROUP, HD)
    key_heads = key_tile.reshape(tile_rows, KVH, HD)
    scores = jnp.einsum(
        "tkgd,skd->kgts", query_heads, key_heads, preferred_element_type=jnp.float32
    ) / math.sqrt(HD)
    scores = jnp.where(keep_mask[None, None], scores, neg_fill)
    attn_probs = jax.nn.softmax(scores, axis=-1)
    probs_b = attn_probs.astype(jnp.bfloat16)
    grad_heads = grad_tile.reshape(tile_rows, KVH, GROUP, HD)
    value_gradient = jnp.einsum(
        "kgts,tkgd->skd", probs_b, grad_heads, preferred_element_type=jnp.float32
    )
    return (attn_probs, probs_b, value_gradient.reshape(tile_rows, KVH * HD).astype(jnp.bfloat16))


def second_pass(attn_probs, probs_b, value_tile, key_tile, grad_tile):
    tile_rows = value_tile.shape[0]
    value_heads = value_tile.reshape(tile_rows, KVH, HD)
    key_heads = key_tile.reshape(tile_rows, KVH, HD)
    grad_heads = grad_tile.reshape(tile_rows, KVH, GROUP, HD)
    out_attn = jnp.einsum(
        "kgts,skd->tkgd", probs_b, value_heads, preferred_element_type=jnp.float32
    )
    dprobs = jnp.einsum(
        "tkgd,skd->kgts", grad_heads, value_heads, preferred_element_type=jnp.float32
    )
    row_delta = jnp.transpose(
        jnp.sum(grad_heads.astype(jnp.float32) * out_attn, axis=-1), (1, 2, 0)
    )[..., None]
    dscores = (attn_probs * (dprobs - row_delta)).astype(jnp.bfloat16)
    grad_heads_q = jnp.einsum(
        "kgts,skd->tkgd", dscores, key_heads, preferred_element_type=jnp.float32
    ) / math.sqrt(HD)
    return grad_heads_q.reshape(tile_rows, KVH * GROUP * HD).astype(jnp.bfloat16)


def local(
    x_rows,
    query_rows,
    key_rows,
    values_base,
    grad_out,
    adapt_down,
    adapt_up,
    block_tenant,
    owner_map,
    seq_ids,
):
    tok_rows = x_rows.shape[0]
    blk_count = block_tenant.shape[0]
    block_len = tok_rows // blk_count
    width = x_rows.shape[1]
    value_width = key_rows.shape[1]
    adapter_count = owner_map.shape[0]
    sliced_down, sliced_up = (
        lax.all_to_all(adapt_down, "dp", split_axis=1, concat_axis=0, tiled=True),
        lax.all_to_all(adapt_up, "dp", split_axis=1, concat_axis=0, tiled=True),
    )
    tenants = lax.all_gather(block_tenant, "dp", axis=0, tiled=True)
    lookup = tenants[:, None] == jnp.arange(adapter_count)[None, :]
    store_rows = jnp.sum(jnp.where(lookup, owner_map[None, :], 0), axis=1)
    picked_down = jnp.take(sliced_down, store_rows, axis=0)
    picked_up = jnp.take(sliced_up, store_rows, axis=0)
    my_down, tenant_up_weight = (
        lax.all_to_all(picked_down, "dp", split_axis=0, concat_axis=1, tiled=True),
        lax.all_to_all(picked_up, "dp", split_axis=0, concat_axis=1, tiled=True),
    )
    tile_rows = min(tok_rows, 512)
    tile_count = tok_rows // tile_rows
    query_tiles = query_rows.reshape(tile_count, tile_rows, -1)
    key_tiles = key_rows.reshape(tile_count, tile_rows, -1)
    grad_tiles = grad_out.reshape(tile_count, tile_rows, -1)
    seq_tiles = seq_ids.reshape(tile_count, tile_rows)
    keep_masks = jax.vmap(lambda ids: build_mask(ids, block_len))(seq_tiles)
    attn_probs, probs_b, value_gradient = jax.vmap(first_pass)(
        query_tiles, key_tiles, grad_tiles, keep_masks
    )
    dvalue_blocks = value_gradient.reshape(blk_count, block_len, value_width)
    x_blocks = x_rows.reshape(blk_count, block_len, width)
    hidden_rows = jnp.einsum(
        "btd,brd->btr", x_blocks, my_down, preferred_element_type=jnp.float32
    ).astype(jnp.bfloat16)
    adapter_values = jnp.einsum(
        "uzd,udv->uzv", hidden_rows, tenant_up_weight, preferred_element_type=jnp.float32
    )
    frozen_value_blocks = values_base.reshape(blk_count, block_len, value_width).astype(jnp.float32)
    value_rows = (frozen_value_blocks + adapter_scale * adapter_values).astype(jnp.bfloat16)
    hidden_gradient = (
        adapter_scale
        * jnp.einsum(
            "bte,bre->btr", dvalue_blocks, tenant_up_weight, preferred_element_type=jnp.float32
        )
    ).astype(jnp.bfloat16)
    part_down = jnp.einsum(
        "btr,btd->brd", hidden_gradient, x_blocks, preferred_element_type=jnp.float32
    )
    partial_up_weight = adapter_scale * jnp.einsum(
        "btr,bte->bre", hidden_rows, dvalue_blocks, preferred_element_type=jnp.float32
    )
    back_down, back_up = (
        lax.all_to_all(part_down, "dp", split_axis=1, concat_axis=0, tiled=True),
        lax.all_to_all(partial_up_weight, "dp", split_axis=1, concat_axis=0, tiled=True),
    )
    selector = (jnp.arange(adapter_count)[:, None] == store_rows[None, :]).astype(jnp.float32)
    sum_down = jnp.einsum("ab,brc->arc", selector, back_down, precision=lax.Precision.HIGHEST)
    sum_up = jnp.einsum("ab,brc->arc", selector, back_up, precision=lax.Precision.HIGHEST)
    grad_down, grad_up = (
        lax.all_to_all(
            sum_down.astype(jnp.bfloat16), "dp", split_axis=0, concat_axis=1, tiled=True
        ),
        lax.all_to_all(sum_up.astype(jnp.bfloat16), "dp", split_axis=0, concat_axis=1, tiled=True),
    )
    local_grad = jnp.einsum(
        "brd,btr->dbt", my_down, hidden_gradient, preferred_element_type=jnp.float32
    )
    local_grad = local_grad.reshape(width, tok_rows).astype(jnp.bfloat16)
    grad_input_t = lax.all_to_all(local_grad, "dp", split_axis=0, concat_axis=1, tiled=True)
    value_tiles = value_rows.reshape(tile_count, tile_rows, value_width)
    grad_query = jax.vmap(second_pass)(attn_probs, probs_b, value_tiles, key_tiles, grad_tiles)
    grad_query = grad_query.reshape(tok_rows, -1)
    return (grad_query, grad_input_t, grad_down, grad_up)


def lane_fold(mask):
    return 4 * ((mask >> 3) ^ (mask & 1)) + ((mask >> 1) & 3)


def pack_kernel(where_ref, tenant_ref, owner_ref, x_ref, down_ref, up_ref, *refs):
    outs, (sems, ids) = refs[:SPAN], refs[SPAN:]
    near, far, pack_ref = outs[: CLUSTER - 1], outs[CLUSTER - 1 : -1], outs[-1]
    part = where_ref[0]
    tok_rows, rank = x_ref.shape[0], down_ref.shape[1]
    span = near[0].shape[1]

    def columns(mask):
        return pl.ds(pl.multiple_of((part ^ lane_fold(mask)) * span, 128), span)

    copies = []
    for mask in range(CLUSTER, SPAN):
        copies.append((down_ref.at[0, :, columns(mask)], far[mask - CLUSTER]))
    for mask in range(1, CLUSTER):
        copies.append((x_ref.at[:, columns(mask)], near[mask - 1].at[pl.ds(0, tok_rows)]))
        copies.append((down_ref.at[0, :, columns(mask)], near[mask - 1].at[pl.ds(tok_rows, rank)]))
    copies = [
        pltpu.make_async_copy(src, dst, sems.at[k]) for k, (src, dst) in enumerate(copies)
    ]
    for copy in copies:
        copy.start()
    pack_ref[pl.ds(0, rank), :] = up_ref[0]
    first = owner_ref[tenant_ref[0]].astype(jnp.float32)
    second = owner_ref[tenant_ref[1]].astype(jnp.float32)
    lane = lax.broadcasted_iota(jnp.int32, ids.shape, 1)
    ids[...] = jnp.where(lane < ids.shape[1] // 2, first, second)
    pack_ref[pl.ds(rank, 16), :] = ids[...].astype(jnp.bfloat16)
    for copy in copies:
        copy.wait()


def first_kernel(ids_ref, query_ref, key_ref, grad_ref, dval_ref, probs_ref):
    step = pl.program_id(0)
    ids = ids_ref[pl.ds(step, 1), :]
    length = ids.shape[1]
    across = jnp.broadcast_to(ids.astype(jnp.float32), (length, length))
    later = lax.broadcasted_iota(jnp.int32, (length, length), 1)
    earlier = lax.broadcasted_iota(jnp.int32, (length, length), 0)
    keep = (across == across.T) & (earlier <= later)
    keys = key_ref[...]
    total = jnp.zeros((length, HD), jnp.float32)
    for head in range(GROUP):
        lanes = pl.ds(head * HD, HD)
        scores = lax.dot_general(
            keys, query_ref[:, lanes], (((1,), (1,)), ((), ())), preferred_element_type=jnp.float32
        ) * (1.0 / math.sqrt(HD))
        scores = jnp.where(keep, scores, neg_fill)
        weights = jnp.exp(scores - jnp.max(scores, axis=0, keepdims=True))
        probs = weights / jnp.sum(weights, axis=0, keepdims=True)
        probs = probs.astype(jnp.bfloat16)
        probs_ref[:, lanes] = probs
        total += jnp.dot(probs, grad_ref[:, lanes], preferred_element_type=jnp.float32)
    dval_ref[...] = total.astype(jnp.bfloat16)


def grad_hidden_kernel(slot_ref, dval_ref, up_ref, out_ref):
    rank = out_ref.shape[0]
    out = lax.dot_general(
        up_ref[0, pl.ds(0, rank), :],
        dval_ref[...],
        (((1,), (1,)), ((), ())),
        preferred_element_type=jnp.float32,
    )
    out_ref[...] = (adapter_scale * out).astype(jnp.bfloat16)


def hidden_kernel(where_ref, store_ref, x_ref, down_ref, *refs):
    near, far = refs[: CLUSTER - 1], refs[CLUSTER - 1 : SPAN - 1]
    outs, all_down, (rows, sems) = refs[SPAN - 1 : -3], refs[-3], refs[-2:]
    part, me = where_ref[0], where_ref[1]
    tok_rows, rank = x_ref.shape[0], down_ref.shape[1]
    span = near[0].shape[1]
    block = tok_rows // 2
    mine = pl.ds(pl.multiple_of(part * span, 128), span)
    copies = [(x_ref.at[:, mine], rows.at[0]), (down_ref.at[0, :, mine], all_down.at[0])]
    for mask in range(CLUSTER, SPAN):
        copies.append((far[mask - CLUSTER], all_down.at[mask]))
    for mask in range(1, CLUSTER):
        copies.append((near[mask - 1].at[pl.ds(0, tok_rows)], rows.at[mask]))
        copies.append((near[mask - 1].at[pl.ds(tok_rows, rank)], all_down.at[mask]))
    copies = [
        pltpu.make_async_copy(src, dst, sems.at[k]) for k, (src, dst) in enumerate(copies)
    ]
    for copy in copies:
        copy.start()
    for copy in copies:
        copy.wait()
    for mask in range(CLUSTER):
        for k in range(2):
            down = all_down[store_ref[mask, k] ^ me]
            out = lax.dot_general(
                down,
                rows[mask, pl.ds(k * block, block), :],
                (((1,), (1,)), ((), ())),
                preferred_element_type=jnp.float32,
            )
            outs[mask][:, pl.ds(k * block, block)] = out.astype(jnp.bfloat16)


def grad_down_kernel(where_ref, store_ref, x_ref, grad_ref, *refs):
    near, (out_ref, rows, total, sems) = refs[: CLUSTER - 1], refs[CLUSTER - 1 :]
    part = where_ref[0]
    tok_rows = x_ref.shape[0]
    span = near[0].shape[1]
    block = tok_rows // 2
    copies = [(x_ref.at[:, pl.ds(pl.multiple_of(part * span, 128), span)], rows.at[0])]
    for mask in range(1, CLUSTER):
        copies.append((near[mask - 1].at[pl.ds(0, tok_rows)], rows.at[mask]))
    copies = [
        pltpu.make_async_copy(src, dst, sems.at[k]) for k, (src, dst) in enumerate(copies)
    ]
    for copy in copies:
        copy.start()
    total[...] = jnp.zeros_like(total)
    for copy in copies:
        copy.wait()
    for mask in range(CLUSTER):
        for k in range(2):
            store = store_ref[mask, k]
            total[store] += jnp.dot(
                grad_ref[mask, :, pl.ds(k * block, block)],
                rows[mask, pl.ds(k * block, block), :],
                preferred_element_type=jnp.float32,
            )
    out_ref[...] = total[...].astype(jnp.bfloat16)


def values_kernel(slot_ref, base_ref, dval_ref, up_ref, *refs):
    hidden_refs, (val_ref, out_ref) = refs[:CLUSTER], refs[CLUSTER:]
    rank = out_ref.shape[1]
    block = base_ref.shape[0] // 2
    hidden = hidden_refs[0][...].astype(jnp.float32)
    for ref in hidden_refs[1:]:
        hidden = hidden + ref[...].astype(jnp.float32)
    hidden = hidden.astype(jnp.bfloat16)
    out_ref[...] = jnp.zeros_like(out_ref)
    terms = []
    for k in range(2):
        rows = pl.ds(k * block, block)
        part = hidden[:, k * block : (k + 1) * block]
        added = lax.dot_general(
            part,
            up_ref[slot_ref[k], pl.ds(0, rank), :],
            (((0,), (0,)), ((), ())),
            preferred_element_type=jnp.float32,
        )
        val_ref[rows, :] = (base_ref[rows, :].astype(jnp.float32) + adapter_scale * added).astype(
            jnp.bfloat16
        )
        terms.append(
            adapter_scale * jnp.dot(part, dval_ref[rows, :], preferred_element_type=jnp.float32)
        )
    same = (slot_ref[0] == slot_ref[1]).astype(jnp.float32)
    out_ref[slot_ref[0]] = terms[0].astype(jnp.bfloat16)
    out_ref[slot_ref[1]] = (terms[1] + same * terms[0]).astype(jnp.bfloat16)


def second_kernel(probs_ref, value_ref, key_ref, grad_ref, out_ref):
    values, keys = value_ref[...], key_ref[...]
    for head in range(GROUP):
        lanes = pl.ds(head * HD, HD)
        probs = probs_ref[:, lanes].astype(jnp.float32)
        dprobs = lax.dot_general(
            values, grad_ref[:, lanes], (((1,), (1,)), ((), ())), preferred_element_type=jnp.float32
        )
        delta = jnp.sum(probs * dprobs, axis=0, keepdims=True)
        dscores = (probs * (dprobs - delta)).astype(jnp.bfloat16)
        out = lax.dot_general(
            dscores, keys, (((0,), (0,)), ((), ())), preferred_element_type=jnp.float32
        )
        out_ref[:, lanes] = (out * (1.0 / math.sqrt(HD))).astype(jnp.bfloat16)


def grad_input_kernel(where_ref, store_ref, grad_ref, own_ref, other_ref, out_ref, down, wide, sem):
    me = where_ref[1]
    core = me & 1
    block = grad_ref.shape[2] // 2
    feats, span = out_ref.shape[0], down.shape[2]
    window = wide.shape[0]

    @pl.when(core == 0)
    def _():
        pltpu.make_async_copy(own_ref, down, sem).start()

    @pl.when(core == 1)
    def _():
        pltpu.make_async_copy(other_ref, down, sem).start()

    pltpu.make_async_copy(own_ref, down, sem).wait()
    lanes = pl.ds(pl.multiple_of(core * (span - window), 128), window)
    skip = pl.ds(pl.multiple_of(core * (window - feats), 16), feats)

    def step(mask, carry):
        for k in range(2):
            part = down[store_ref[mask, k] ^ (me & ~1), :, lanes]
            wide[...] = lax.dot_general(
                part,
                grad_ref[mask, :, pl.ds(k * block, block)],
                (((0,), (0,)), ((), ())),
                preferred_element_type=jnp.float32,
            )
            at = pl.multiple_of(((mask ^ me) * 2 + k) * block, 128)
            out_ref[:, pl.ds(at, block)] = wide[skip, :].astype(jnp.bfloat16)
        return carry

    lax.fori_loop(0, SPAN, step, 0)


def swap(value, mask):
    return lax.ppermute(value, "dp", [(i, i ^ mask) for i in range(SPAN)])


def spread(value):
    value = value[None]
    for mask in (8, 4, 2, 1):
        value = jnp.stack([value, swap(value, mask)], axis=1)
        value = value.reshape((-1,) + value.shape[2:])
    return value


def local_clustered(
    x_rows,
    query_rows,
    key_rows,
    values_base,
    grad_out,
    adapt_down,
    adapt_up,
    block_tenant,
    owner_map,
    seq_ids,
):
    tok_rows, width = x_rows.shape
    value_width = key_rows.shape[1]
    query_width = query_rows.shape[1]
    rank = adapt_down.shape[1]
    blocks, block = seq_ids.shape
    heads = value_width // HD
    span = width // CLUSTER
    group_width = GROUP * HD
    bf16, f32 = jnp.bfloat16, jnp.float32
    any_spec = pl.BlockSpec(memory_space=pl.ANY)
    smem_spec = pl.BlockSpec(memory_space=pltpu.SMEM)
    vmem_spec = pl.BlockSpec(memory_space=pltpu.VMEM)
    shape = jax.ShapeDtypeStruct
    params = pltpu.CompilerParams(vmem_limit_bytes=48 * 1024 * 1024)

    me = lax.axis_index("dp")
    part = 4 * ((me >> 3) ^ (me & 1)) + ((me >> 1) & 3)
    where = jnp.stack([part, me]).astype(jnp.int32)

    packed = pl.pallas_call(
        pack_kernel,
        in_specs=[smem_spec] * 3 + [any_spec] * 2 + [vmem_spec],
        out_specs=[any_spec] * (SPAN - 1) + [vmem_spec],
        out_shape=[shape((tok_rows + rank, span), bf16)] * (CLUSTER - 1)
        + [shape((rank, span), bf16)] * CLUSTER
        + [shape((rank + 16, value_width), bf16)],
        scratch_shapes=[
            pltpu.SemaphoreType.DMA((3 * CLUSTER,)),
            pltpu.VMEM((16, value_width), f32),
        ],
        compiler_params=params,
        name="pack",
    )(where, block_tenant, owner_map, x_rows, adapt_down, adapt_up)
    near, far, up_pack = packed[: CLUSTER - 1], packed[CLUSTER - 1 : -1], packed[-1]
    far = [swap(far[m - CLUSTER], m) for m in range(CLUSTER, SPAN)]
    near = [swap(near[m - 1], m) for m in range(1, CLUSTER)]

    dvalues, probs = pl.pallas_call(
        first_kernel,
        grid=(blocks, heads),
        in_specs=[
            vmem_spec,
            pl.BlockSpec((block, group_width), lambda b, h: (b, h)),
            pl.BlockSpec((block, HD), lambda b, h: (b, h)),
            pl.BlockSpec((block, group_width), lambda b, h: (b, h)),
        ],
        out_specs=[
            pl.BlockSpec((block, HD), lambda b, h: (b, h)),
            pl.BlockSpec((block, group_width), lambda b, h: (b, h)),
        ],
        out_shape=[shape((tok_rows, value_width), bf16), shape((tok_rows, query_width), bf16)],
        compiler_params=params,
        cost_estimate=pl.CostEstimate(
            flops=4 * tok_rows * query_width * block, bytes_accessed=3 * tok_rows * query_width * 2, transcendentals=0
        ),
        name="first_pass",
    )(seq_ids, query_rows, key_rows, grad_out)

    all_up = spread(up_pack)
    stores = jnp.stack([all_up[:, rank, 0], all_up[:, rank, value_width // 2]], axis=1)
    stores = stores.astype(jnp.int32)
    slots = stores[0] ^ me

    hidden_gradient = pl.pallas_call(
        grad_hidden_kernel,
        grid_spec=pltpu.PrefetchScalarGridSpec(
            num_scalar_prefetch=1,
            grid=(blocks,),
            in_specs=[
                pl.BlockSpec((block, value_width), lambda b, slot: (b, 0)),
                pl.BlockSpec((1, rank + 16, value_width), lambda b, slot: (slot[b], 0, 0)),
            ],
            out_specs=pl.BlockSpec((rank, block), lambda b, slot: (0, b)),
        ),
        out_shape=shape((rank, tok_rows), bf16),
        compiler_params=params,
        name="grad_hidden",
    )(slots, dvalues, all_up)
    all_grad = spread(hidden_gradient)

    hidden_parts = pl.pallas_call(
        hidden_kernel,
        in_specs=[smem_spec] * 2 + [any_spec] * (SPAN + 1),
        out_specs=[vmem_spec] * (CLUSTER + 1),
        out_shape=[shape((rank, tok_rows), bf16)] * CLUSTER + [shape((SPAN, rank, span), bf16)],
        scratch_shapes=[
            pltpu.VMEM((CLUSTER, tok_rows, span), bf16),
            pltpu.SemaphoreType.DMA((3 * CLUSTER,)),
        ],
        compiler_params=params,
        name="hidden",
    )(where, stores, x_rows, adapt_down, *near, *far)
    all_down = hidden_parts[-1]
    hidden_parts = [hidden_parts[0]] + [swap(hidden_parts[m], m) for m in range(1, CLUSTER)]
    other_down = lax.ppermute(all_down, "dp", [(i, i + 1) for i in range(0, SPAN, 2)])

    down_parts = pl.pallas_call(
        grad_down_kernel,
        in_specs=[smem_spec] * 2 + [any_spec, vmem_spec] + [any_spec] * (CLUSTER - 1),
        out_specs=vmem_spec,
        out_shape=shape((SPAN, rank, span), bf16),
        scratch_shapes=[
            pltpu.VMEM((CLUSTER, tok_rows, span), bf16),
            pltpu.VMEM((SPAN, rank, span), f32),
            pltpu.SemaphoreType.DMA((CLUSTER,)),
        ],
        compiler_params=params,
        name="grad_down",
    )(where, stores, x_rows, all_grad[:CLUSTER], *near)
    down_parts = lax.all_to_all(down_parts, "dp", split_axis=0, concat_axis=0, tiled=True)

    value_rows, up_parts = pl.pallas_call(
        values_kernel,
        in_specs=[smem_spec] + [vmem_spec] * (3 + CLUSTER),
        out_specs=[vmem_spec] * 2,
        out_shape=[shape((tok_rows, value_width), bf16), shape((SPAN, rank, value_width), bf16)],
        compiler_params=params,
        name="values",
    )(slots, values_base, dvalues, all_up, *hidden_parts)

    for mask in (1, 2, 4, 8):
        pair = up_parts.reshape((-1, 2) + up_parts.shape[1:])
        up_parts = (pair[:, 0].astype(f32) + swap(pair[:, 1], mask).astype(f32)).astype(bf16)
    grad_up = up_parts

    grad_query = pl.pallas_call(
        second_kernel,
        grid=(blocks, heads),
        in_specs=[
            pl.BlockSpec((block, group_width), lambda b, h: (b, h)),
            pl.BlockSpec((block, HD), lambda b, h: (b, h)),
            pl.BlockSpec((block, HD), lambda b, h: (b, h)),
            pl.BlockSpec((block, group_width), lambda b, h: (b, h)),
        ],
        out_specs=pl.BlockSpec((block, group_width), lambda b, h: (b, h)),
        out_shape=shape((tok_rows, query_width), bf16),
        compiler_params=params,
        cost_estimate=pl.CostEstimate(
            flops=4 * tok_rows * query_width * block, bytes_accessed=3 * tok_rows * query_width * 2, transcendentals=0
        ),
        name="second_pass",
    )(probs, value_rows, key_rows, grad_out)

    feats = width // SPAN
    window = -(-feats // 128) * 128
    grad_input_t = pl.pallas_call(
        grad_input_kernel,
        in_specs=[smem_spec] * 2 + [vmem_spec] + [any_spec] * 2,
        out_specs=vmem_spec,
        out_shape=shape((feats, SPAN * tok_rows), bf16),
        scratch_shapes=[
            pltpu.VMEM((SPAN, rank, span), bf16),
            pltpu.VMEM((window, block), f32),
            pltpu.SemaphoreType.DMA,
        ],
        compiler_params=params,
        name="grad_input",
    )(where, stores, all_grad, all_down, other_down)

    order = [[i for i in range(SPAN) if lane_fold(i) == p] for p in range(CLUSTER)]
    grad_down = jnp.concatenate(
        [down_parts[a].astype(f32) + down_parts[b].astype(f32) for a, b in order], axis=1
    ).astype(bf16)
    return (grad_query, grad_input_t, grad_down[None], grad_up)


def solution(mesh):
    clustered = mesh.shape["dp"] == SPAN
    in_specs = (
        P(("groups", "dp"), None),
        P(("groups", "dp"), None),
        P(("groups", "dp"), None),
        P(("groups", "dp"), None),
        P(("groups", "dp"), None),
        P("dp", None, None),
        P("dp", None, None),
        P(("groups", "dp")),
        P(),
        P(("groups", "dp"), None),
    )
    out_specs = (
        P(("groups", "dp"), None),
        P("dp", "groups"),
        P(("groups", "dp"), None, None),
        P(("groups", "dp"), None, None),
    )
    return jax.shard_map(
        local_clustered if clustered else local, mesh=mesh, in_specs=in_specs, out_specs=out_specs, check_vma=False
    )
```

```python
import math

import jax
import jax.numpy as jnp
from jax import lax
from jax.experimental import pallas as pl
from jax.experimental.pallas import tpu as pltpu
from jax.sharding import PartitionSpec as P

HD = 128
KVH = 4
GROUP = 8
CHIPS = 4
SPAN = 16


adapter_scale = 2.0
neg_fill = -1e30


def build_mask(seg_ids, block_len):
    position = jnp.arange(seg_ids.shape[0])
    block_ids = position // block_len
    same_block = block_ids[:, None] == block_ids[None, :]
    same_seq = seg_ids[:, None] == seg_ids[None, :]
    causal = position[None, :] <= position[:, None]
    return same_block & same_seq & causal


def first_pass(query_tile, key_tile, grad_tile, keep_mask):
    tile_rows = query_tile.shape[0]
    query_heads = query_tile.reshape(tile_rows, KVH, GROUP, HD)
    key_heads = key_tile.reshape(tile_rows, KVH, HD)
    scores = jnp.einsum(
        "tkgd,skd->kgts", query_heads, key_heads, preferred_element_type=jnp.float32
    ) / math.sqrt(HD)
    scores = jnp.where(keep_mask[None, None], scores, neg_fill)
    attn_probs = jax.nn.softmax(scores, axis=-1)
    probs_b = attn_probs.astype(jnp.bfloat16)
    grad_heads = grad_tile.reshape(tile_rows, KVH, GROUP, HD)
    value_gradient = jnp.einsum(
        "kgts,tkgd->skd", probs_b, grad_heads, preferred_element_type=jnp.float32
    )
    return (attn_probs, probs_b, value_gradient.reshape(tile_rows, KVH * HD).astype(jnp.bfloat16))


def second_pass(attn_probs, probs_b, value_tile, key_tile, grad_tile):
    tile_rows = value_tile.shape[0]
    value_heads = value_tile.reshape(tile_rows, KVH, HD)
    key_heads = key_tile.reshape(tile_rows, KVH, HD)
    grad_heads = grad_tile.reshape(tile_rows, KVH, GROUP, HD)
    out_attn = jnp.einsum(
        "kgts,skd->tkgd", probs_b, value_heads, preferred_element_type=jnp.float32
    )
    dprobs = jnp.einsum(
        "tkgd,skd->kgts", grad_heads, value_heads, preferred_element_type=jnp.float32
    )
    row_delta = jnp.transpose(
        jnp.sum(grad_heads.astype(jnp.float32) * out_attn, axis=-1), (1, 2, 0)
    )[..., None]
    dscores = (attn_probs * (dprobs - row_delta)).astype(jnp.bfloat16)
    grad_heads_q = jnp.einsum(
        "kgts,skd->tkgd", dscores, key_heads, preferred_element_type=jnp.float32
    ) / math.sqrt(HD)
    return grad_heads_q.reshape(tile_rows, KVH * GROUP * HD).astype(jnp.bfloat16)


def local(
    x_rows,
    query_rows,
    key_rows,
    values_base,
    grad_out,
    adapt_down,
    adapt_up,
    block_tenant,
    owner_map,
    seq_ids,
):
    tok_rows = x_rows.shape[0]
    blk_count = block_tenant.shape[0]
    block_len = tok_rows // blk_count
    width = x_rows.shape[1]
    value_width = key_rows.shape[1]
    adapter_count = owner_map.shape[0]
    sliced_down, sliced_up = (
        lax.all_to_all(adapt_down, "dp", split_axis=1, concat_axis=0, tiled=True),
        lax.all_to_all(adapt_up, "dp", split_axis=1, concat_axis=0, tiled=True),
    )
    tenants = lax.all_gather(block_tenant, "dp", axis=0, tiled=True)
    lookup = tenants[:, None] == jnp.arange(adapter_count)[None, :]
    store_rows = jnp.sum(jnp.where(lookup, owner_map[None, :], 0), axis=1)
    picked_down = jnp.take(sliced_down, store_rows, axis=0)
    picked_up = jnp.take(sliced_up, store_rows, axis=0)
    my_down, tenant_up_weight = (
        lax.all_to_all(picked_down, "dp", split_axis=0, concat_axis=1, tiled=True),
        lax.all_to_all(picked_up, "dp", split_axis=0, concat_axis=1, tiled=True),
    )
    tile_rows = min(tok_rows, 512)
    tile_count = tok_rows // tile_rows
    query_tiles = query_rows.reshape(tile_count, tile_rows, -1)
    key_tiles = key_rows.reshape(tile_count, tile_rows, -1)
    grad_tiles = grad_out.reshape(tile_count, tile_rows, -1)
    seq_tiles = seq_ids.reshape(tile_count, tile_rows)
    keep_masks = jax.vmap(lambda ids: build_mask(ids, block_len))(seq_tiles)
    attn_probs, probs_b, value_gradient = jax.vmap(first_pass)(
        query_tiles, key_tiles, grad_tiles, keep_masks
    )
    dvalue_blocks = value_gradient.reshape(blk_count, block_len, value_width)
    x_blocks = x_rows.reshape(blk_count, block_len, width)
    hidden_rows = jnp.einsum(
        "btd,brd->btr", x_blocks, my_down, preferred_element_type=jnp.float32
    ).astype(jnp.bfloat16)
    adapter_values = jnp.einsum(
        "uzd,udv->uzv", hidden_rows, tenant_up_weight, preferred_element_type=jnp.float32
    )
    frozen_value_blocks = values_base.reshape(blk_count, block_len, value_width).astype(jnp.float32)
    value_rows = (frozen_value_blocks + adapter_scale * adapter_values).astype(jnp.bfloat16)
    hidden_gradient = (
        adapter_scale
        * jnp.einsum(
            "bte,bre->btr", dvalue_blocks, tenant_up_weight, preferred_element_type=jnp.float32
        )
    ).astype(jnp.bfloat16)
    part_down = jnp.einsum(
        "btr,btd->brd", hidden_gradient, x_blocks, preferred_element_type=jnp.float32
    )
    partial_up_weight = adapter_scale * jnp.einsum(
        "btr,bte->bre", hidden_rows, dvalue_blocks, preferred_element_type=jnp.float32
    )
    back_down, back_up = (
        lax.all_to_all(part_down, "dp", split_axis=1, concat_axis=0, tiled=True),
        lax.all_to_all(partial_up_weight, "dp", split_axis=1, concat_axis=0, tiled=True),
    )
    selector = (jnp.arange(adapter_count)[:, None] == store_rows[None, :]).astype(jnp.float32)
    sum_down = jnp.einsum("ab,brc->arc", selector, back_down, precision=lax.Precision.HIGHEST)
    sum_up = jnp.einsum("ab,brc->arc", selector, back_up, precision=lax.Precision.HIGHEST)
    grad_down, grad_up = (
        lax.all_to_all(
            sum_down.astype(jnp.bfloat16), "dp", split_axis=0, concat_axis=1, tiled=True
        ),
        lax.all_to_all(sum_up.astype(jnp.bfloat16), "dp", split_axis=0, concat_axis=1, tiled=True),
    )
    local_grad = jnp.einsum(
        "brd,btr->dbt", my_down, hidden_gradient, preferred_element_type=jnp.float32
    )
    local_grad = local_grad.reshape(width, tok_rows).astype(jnp.bfloat16)
    grad_input_t = lax.all_to_all(local_grad, "dp", split_axis=0, concat_axis=1, tiled=True)
    value_tiles = value_rows.reshape(tile_count, tile_rows, value_width)
    grad_query = jax.vmap(second_pass)(attn_probs, probs_b, value_tiles, key_tiles, grad_tiles)
    grad_query = grad_query.reshape(tok_rows, -1)
    return (grad_query, grad_input_t, grad_down, grad_up)


def cost(micros):
    return pl.CostEstimate(flops=0, bytes_accessed=int(micros * 3.3e4), transcendentals=0)


def eighth_of(device):
    return 4 * ((device >> 3) ^ (device & 1)) + ((device >> 1) & 3)


def run_copies(pairs, sems):
    copies = [pltpu.make_async_copy(src, dst, sems.at[k]) for k, (src, dst) in enumerate(pairs)]
    for copy in copies:
        copy.start()
    return copies


def columns(part, span):
    return pl.ds(pl.multiple_of(part * span, 128), span)


def pack_kernel(x_ref, down_ref, down_out, *refs):
    outs, (x_buf, down_buf, sems) = refs[: CHIPS - 1], refs[CHIPS - 1 :]
    me, group = lax.axis_index("dp"), lax.axis_index("groups")
    half, span = down_out.shape[1:]
    ranks = pl.ds(pl.multiple_of(group * half, 16), half)
    pairs = []
    for k in range(CHIPS - 1):
        chip = ((me >> 1) & 3) ^ (k + 1)
        for side in range(2):
            part = 4 * ((me >> 3) ^ side) + chip
            pairs.append((x_ref.at[:, columns(part, span)], x_buf.at[k, :, pl.ds(side * span, span)]))
    pairs.append((down_ref.at[0, ranks, :], down_buf))
    loads = run_copies(pairs, sems)
    pairs = [(x_buf.at[k], outs[k]) for k in range(CHIPS - 1)]
    for dest in range(SPAN):
        pairs.append((down_buf.at[:, pl.ds(eighth_of(dest) * span, span)], down_out.at[dest]))
    stores = [
        pltpu.make_async_copy(src, dst, sems.at[len(loads) + k])
        for k, (src, dst) in enumerate(pairs)
    ]
    for k in range(CHIPS - 1):
        loads[2 * k].wait()
        loads[2 * k + 1].wait()
        stores[k].start()
    loads[-1].wait()
    for copy in stores[CHIPS - 1 :]:
        copy.start()
    for copy in stores:
        copy.wait()


def store_kernel(tenant_ref, owner_ref, slot_ref, row_ref, wide):
    for k in range(2):
        slot_ref[k] = owner_ref[tenant_ref[k]]
    lane = lax.broadcasted_iota(jnp.int32, wide.shape, 1)
    wide[...] = jnp.where(
        lane < wide.shape[1] // 2, slot_ref[0].astype(jnp.float32), slot_ref[1].astype(jnp.float32)
    )
    row_ref[...] = wide[...].astype(jnp.bfloat16)


def heads_in_rows(ref):
    return jnp.concatenate([ref[:, h * HD : (h + 1) * HD] for h in range(GROUP)], axis=0)


def probabilities(ids, keys, queries):
    length = ids.shape[1]
    across = jnp.broadcast_to(ids.astype(jnp.float32), (length, length))
    later = lax.broadcasted_iota(jnp.int32, (length, length), 1)
    earlier = lax.broadcasted_iota(jnp.int32, (length, length), 0)
    keep = (across == across.T) & (earlier <= later)
    scores = lax.dot_general(
        keys, queries, (((1,), (1,)), ((), ())), preferred_element_type=jnp.float32
    ) * (1.0 / math.sqrt(HD))
    scores = jnp.where(jnp.concatenate([keep] * GROUP, axis=1), scores, neg_fill)
    weights = jnp.exp(scores - jnp.max(scores, axis=0, keepdims=True))
    return weights * (1.0 / jnp.sum(weights, axis=0, keepdims=True))


def first_kernel(ids_ref, query_ref, key_ref, grad_ref, dval_ref):
    ids = ids_ref[pl.ds(pl.program_id(0), 1), :]
    probs = probabilities(ids, key_ref[...], heads_in_rows(query_ref)).astype(jnp.bfloat16)
    out = jnp.dot(probs, heads_in_rows(grad_ref), preferred_element_type=jnp.float32)
    dval_ref[...] = out.astype(jnp.bfloat16)


def second_kernel(ids_ref, query_ref, key_ref, value_ref, grad_ref, out_ref):
    ids = ids_ref[pl.ds(pl.program_id(0), 1), :]
    keys = key_ref[...]
    probs = probabilities(ids, keys, heads_in_rows(query_ref))
    dprobs = lax.dot_general(
        value_ref[...],
        heads_in_rows(grad_ref),
        (((1,), (1,)), ((), ())),
        preferred_element_type=jnp.float32,
    )
    rounded = probs.astype(jnp.bfloat16).astype(jnp.float32)
    delta = jnp.sum(rounded * dprobs, axis=0, keepdims=True)
    dscores = (probs * (dprobs - delta)).astype(jnp.bfloat16)
    turned = keys.astype(jnp.float32).T.astype(jnp.bfloat16)
    out = jnp.dot(turned, dscores, preferred_element_type=jnp.float32) * (1.0 / math.sqrt(HD))
    for head in range(GROUP):
        lanes = slice(head * HD, (head + 1) * HD)
        out_ref[:, lanes] = out[:, lanes].T.astype(jnp.bfloat16)


def grad_hidden_kernel(slot_ref, dval_ref, up_ref, *refs):
    out_ref = refs[-1]
    rank = out_ref.shape[0]
    out = lax.dot_general(
        up_ref[0],
        dval_ref[...],
        (((1,), (1,)), ((), ())),
        preferred_element_type=jnp.float32,
    )
    out_ref[...] = (adapter_scale * out).astype(jnp.bfloat16)


def x_copies(x_ref, near, rows):
    me = lax.axis_index("dp")
    chip = (me >> 1) & 3
    span = rows.shape[2] // 2
    pairs = []
    for side in range(2):
        part = 4 * ((me >> 3) ^ side) + chip
        pairs.append((x_ref.at[:, columns(part, span)], rows.at[0, :, pl.ds(side * span, span)]))
    for k, ref in enumerate(near):
        pairs.append((ref, rows.at[k + 1]))
    return pairs


def hidden_kernel(store_ref, x_ref, *refs):
    near, downs, outs, (rows, down, sems) = refs[:3], refs[3:7], refs[7:11], refs[11:]
    me, group = lax.axis_index("dp"), lax.axis_index("groups")
    core = me & 1
    span, half = downs[0].shape[2], downs[0].shape[1]
    block = x_ref.shape[0] // 2
    pairs = x_copies(x_ref, near, rows)
    for slot in range(CHIPS):
        for k in range(2):
            store = store_ref[slot, k]
            for kind, ref in enumerate(downs):
                ranks = pl.ds(pl.multiple_of((group ^ (kind & 1)) * half, 16), half)
                lanes = columns(core ^ (kind >> 1), span)
                pairs.append((ref.at[store], down.at[2 * slot + k, ranks, lanes]))
    for copy in run_copies(pairs, sems):
        copy.wait()
    for slot in range(CHIPS):
        for k in range(2):
            out = lax.dot_general(
                down[2 * slot + k],
                rows[slot, pl.ds(k * block, block), :],
                (((1,), (1,)), ((), ())),
                preferred_element_type=jnp.float32,
            )
            outs[slot][:, pl.ds(k * block, block)] = out.astype(jnp.bfloat16)


def grad_down_kernel(store_ref, x_ref, grad_ref, *refs):
    near, (keep_ref, send_ref, rows, total, sems) = refs[:3], refs[5:]
    me = lax.axis_index("dp")
    core = me & 1
    span = keep_ref.shape[2]
    block = x_ref.shape[0] // 2
    copies = run_copies(x_copies(x_ref, near, rows), sems)
    total[...] = jnp.zeros_like(total)
    for copy in copies:
        copy.wait()
    for slot in range(CHIPS):
        for k in range(2):
            store = store_ref[slot, k]
            total[store] += jnp.dot(
                grad_ref[slot, :, pl.ds(k * block, block)],
                rows[slot, pl.ds(k * block, block), :],
                preferred_element_type=jnp.float32,
            )
    keep_ref[...] = total[:, :, columns(core, span)].astype(jnp.bfloat16)
    send_ref[...] = total[:, :, columns(1 - core, span)].astype(jnp.bfloat16)


def sum_kernel(one_ref, two_ref, out_ref):
    out = one_ref[0].astype(jnp.float32) + two_ref[0].astype(jnp.float32)
    out_ref[0] = out.astype(jnp.bfloat16)


def values_kernel(slot_ref, up_slot_ref, base_ref, dval_ref, up_ref, *refs):
    hidden_refs, (val_ref, keep_ref, send_ref) = refs[:CHIPS], refs[CHIPS:]
    rank = keep_ref.shape[1]
    block = base_ref.shape[0] // 2
    hidden = hidden_refs[0][...].astype(jnp.float32)
    for ref in hidden_refs[1:]:
        hidden = hidden + ref[...].astype(jnp.float32)
    hidden = hidden.astype(jnp.bfloat16)
    keep_ref[...] = jnp.zeros_like(keep_ref)
    send_ref[...] = jnp.zeros_like(send_ref)
    terms = []
    for k in range(2):
        rows = pl.ds(k * block, block)
        part = hidden[:, k * block : (k + 1) * block]
        added = lax.dot_general(
            part,
            up_ref[up_slot_ref[k]],
            (((0,), (0,)), ((), ())),
            preferred_element_type=jnp.float32,
        )
        val_ref[rows, :] = (base_ref[rows, :].astype(jnp.float32) + adapter_scale * added).astype(
            jnp.bfloat16
        )
        terms.append(
            adapter_scale * jnp.dot(part, dval_ref[rows, :], preferred_element_type=jnp.float32)
        )
    same = (slot_ref[0] == slot_ref[1]).astype(jnp.float32)
    terms[1] = terms[1] + same * terms[0]
    for k in range(2):
        for side, ref in enumerate((keep_ref, send_ref)):

            @pl.when((slot_ref[k] & 1) == side)
            def _():
                ref[slot_ref[k] >> 1] = terms[k].astype(ref.dtype)


def halve_kernel(kept_ref, came_ref, *outs):
    for k in range(kept_ref.shape[0]):
        ref = outs[k % len(outs)]
        ref[k // len(outs)] = (kept_ref[k] + came_ref[k].astype(jnp.float32)).astype(ref.dtype)


def grad_input_kernel(store_ref, grad_ref, *refs):
    downs, (out_ref, down, wide, turned, sems) = refs[:4], refs[4:]
    me, group = lax.axis_index("dp"), lax.axis_index("groups")
    core = me & 1
    block = grad_ref.shape[2] // 2
    feats, span = out_ref.shape[0], down.shape[2]
    half = down.shape[1] // 2
    window = wide.shape[0]

    def places(kind):
        ranks = pl.ds(pl.multiple_of((group ^ kind) * half, 16), half)
        return down.at[:, ranks, :]

    for side in range(2):

        @pl.when(core == side)
        def _():
            for kind in range(2):
                src = downs[2 * side + kind]
                pltpu.make_async_copy(src, places(kind), sems.at[kind]).start()

    for kind in range(2):
        pltpu.make_async_copy(downs[kind], places(kind), sems.at[kind]).wait()
    lanes = pl.ds(pl.multiple_of(core * (span - window), 128), window)
    skip = pl.ds(pl.multiple_of(core * (window - feats), 16), feats)
    for store in range(SPAN):
        wide[...] = down[store, :, lanes].astype(jnp.float32).T
        turned[store] = wide[skip, :].astype(jnp.bfloat16)
    for mask in range(SPAN):
        for k in range(2):
            out = jnp.dot(
                turned[store_ref[mask, k]],
                grad_ref[mask, :, pl.ds(k * block, block)],
                preferred_element_type=jnp.float32,
            )
            at = pl.multiple_of(((mask ^ me) * 2 + k) * block, 128)
            out_ref[:, pl.ds(at, block)] = out.astype(jnp.bfloat16)


def together(*values):
    return lax.optimization_barrier(values)


def swap(value, mask):
    return lax.ppermute(value, "dp", [(i, i ^ mask) for i in range(SPAN)])


def spread(value, masks, done=()):
    for mask in masks:
        axis = sum(other > mask for other in done)
        value = jnp.stack([value, swap(value, mask)], axis=axis)
        done = done + (mask,)
    return value


def local_clustered(
    x_rows,
    query_rows,
    key_rows,
    values_base,
    grad_out,
    adapt_down,
    adapt_up,
    block_tenant,
    owner_map,
    seq_ids,
):
    tok_rows, width = x_rows.shape
    value_width = key_rows.shape[1]
    query_width = query_rows.shape[1]
    rank = adapt_down.shape[1]
    blocks, block = seq_ids.shape
    heads = value_width // HD
    span = width // (2 * CHIPS)
    group_width = GROUP * HD
    bf16, f32 = jnp.bfloat16, jnp.float32
    any_spec = pl.BlockSpec(memory_space=pltpu.HBM)
    smem_spec = pl.BlockSpec(memory_space=pltpu.SMEM)
    vmem_spec = pl.BlockSpec(memory_space=pltpu.VMEM)
    shape = jax.ShapeDtypeStruct
    params = pltpu.CompilerParams(vmem_limit_bytes=32 * 1024 * 1024)
    big = pltpu.CompilerParams(vmem_limit_bytes=60 * 1024 * 1024)
    wide_spec = pl.BlockSpec((block, group_width), lambda b, h: (b, h))
    head_spec = pl.BlockSpec((block, HD), lambda b, h: (b, h))

    down_pack, *x_packs = pl.pallas_call(
        pack_kernel,
        in_specs=[any_spec] * 2,
        out_specs=[any_spec] * CHIPS,
        out_shape=[shape((SPAN, rank // 2, span), bf16)]
        + [shape((tok_rows, 2 * span), bf16)] * (CHIPS - 1),
        scratch_shapes=[
            pltpu.VMEM((CHIPS - 1, tok_rows, 2 * span), bf16),
            pltpu.VMEM((rank // 2, width), bf16),
            pltpu.SemaphoreType.DMA((SPAN + 3 * CHIPS,)),
        ],
        compiler_params=big,
        cost_estimate=cost(2.5),
        name="pack",
    )(x_rows, adapt_down)

    slots, slot_rows = pl.pallas_call(
        store_kernel,
        in_specs=[smem_spec] * 2,
        out_specs=[smem_spec, vmem_spec],
        out_shape=[shape((blocks,), jnp.int32), shape((16, value_width), bf16)],
        scratch_shapes=[pltpu.VMEM((16, value_width), f32)],
        compiler_params=params,
        name="store_rows",
    )(block_tenant, owner_map)

    dvalues = pl.pallas_call(
        first_kernel,
        grid=(blocks, heads),
        in_specs=[vmem_spec, wide_spec, head_spec, wide_spec],
        out_specs=head_spec,
        out_shape=shape((tok_rows, value_width), bf16),
        compiler_params=params,
        cost_estimate=cost(7),
        name="first_pass",
    )(seq_ids, query_rows, key_rows, grad_out)

    up_pair = jnp.concatenate(
        [jnp.concatenate([value, swap(value, 8)]) for value in (adapt_up[0], slot_rows)]
    )
    x_packs[0], x_packs[1], x_packs[2], up_pair = together(*x_packs, up_pair)
    near_up = jnp.stack([up_pair] + [swap(up_pair, 2 * k) for k in range(1, CHIPS)])
    down_pack, near_up = together(down_pack, near_up)
    near = [swap(x_packs[k], 2 * (k + 1)) for k in range(CHIPS - 1)]
    down_own = lax.all_to_all(down_pack, "dp", split_axis=0, concat_axis=0, tiled=True)
    all_up = jnp.stack([near_up, swap(near_up, 1)])
    stores = all_up[:, :, 2 * rank :].reshape(2, CHIPS, 2, 16, 2, -1)[:, :, :, 0, :, 0]
    stores = stores.astype(jnp.int32)
    near_stores = stores[0, :, 0]
    stores = stores.transpose(2, 1, 0, 3).reshape(SPAN, blocks)
    all_up = all_up[:, :, : 2 * rank].reshape((SPAN,) + adapt_up.shape[1:])
    down_other = lax.ppermute(down_own, "groups", [(0, 1), (1, 0)])
    me = lax.axis_index("dp")
    slots = slots ^ me
    up_slots = 8 * (slots & 1) + 2 * ((slots >> 1) & 3) + (slots >> 3)

    hidden_gradient = pl.pallas_call(
        grad_hidden_kernel,
        grid_spec=pltpu.PrefetchScalarGridSpec(
            num_scalar_prefetch=1,
            grid=(blocks,),
            in_specs=[
                pl.BlockSpec((block, value_width), lambda b, slot: (b, 0)),
                pl.BlockSpec((1, rank, value_width), lambda b, slot: (slot[b], 0, 0)),
                any_spec,
                any_spec,
            ],
            out_specs=pl.BlockSpec((rank, block), lambda b, slot: (0, b)),
        ),
        out_shape=shape((rank, tok_rows), bf16),
        compiler_params=params,
        cost_estimate=cost(1),
        name="grad_hidden",
    )(up_slots, dvalues, all_up, *near[:2])
    far_gradient = swap(hidden_gradient, 8)
    near_grad, far_grad = [
        jnp.stack([grad] + [swap(grad, 2 * k) for k in range(1, CHIPS)])
        for grad in (hidden_gradient, far_gradient)
    ]
    all_grad = jnp.stack([near_grad, far_grad])
    all_grad = jnp.stack([all_grad, swap(all_grad, 1)], axis=2)
    all_grad = all_grad.reshape((SPAN,) + hidden_gradient.shape)

    downs = [down_own, down_other, swap(down_own, 1), swap(down_other, 1)]

    down_keep, down_send = pl.pallas_call(
        grad_down_kernel,
        in_specs=[smem_spec, any_spec, vmem_spec] + [any_spec] * (CHIPS + 1),
        out_specs=[vmem_spec] * 2,
        out_shape=[shape((SPAN, rank, span), bf16)] * 2,
        scratch_shapes=[
            pltpu.VMEM((CHIPS, tok_rows, 2 * span), bf16),
            pltpu.VMEM((SPAN, rank, 2 * span), f32),
            pltpu.SemaphoreType.DMA((CHIPS + 1,)),
        ],
        compiler_params=params,
        cost_estimate=cost(3),
        name="grad_down",
    )(near_stores, x_rows, near_grad, *near, down_other, downs[2])
    hidden_parts = pl.pallas_call(
        hidden_kernel,
        in_specs=[smem_spec] + [any_spec] * (CHIPS + 4),
        out_specs=[vmem_spec] * CHIPS,
        out_shape=[shape((rank, tok_rows), bf16)] * CHIPS,
        scratch_shapes=[
            pltpu.VMEM((CHIPS, tok_rows, 2 * span), bf16),
            pltpu.VMEM((2 * CHIPS, rank, 2 * span), bf16),
            pltpu.SemaphoreType.DMA((9 * CHIPS + 1,)),
        ],
        compiler_params=params,
        cost_estimate=cost(3),
        name="hidden",
    )(near_stores, x_rows, *near, *downs)
    own_part = hidden_parts[0]
    hidden_parts = [own_part] + [swap(hidden_parts[k], 2 * k) for k in range(1, CHIPS)]

    down_parts = (down_keep.astype(f32) + swap(down_send, 1).astype(f32)).astype(bf16)
    down_parts = lax.all_to_all(down_parts, "dp", split_axis=0, concat_axis=0, tiled=True)

    value_rows, kept, sent = pl.pallas_call(
        values_kernel,
        in_specs=[smem_spec] * 2 + [vmem_spec] * (3 + CHIPS),
        out_specs=[vmem_spec] * 3,
        out_shape=[
            shape((tok_rows, value_width), bf16),
            shape((SPAN // 2, rank, value_width), f32),
            shape((SPAN // 2, rank, value_width), bf16),
        ],
        compiler_params=params,
        cost_estimate=cost(1),
        name="values",
    )(slots, up_slots, values_base, dvalues, all_up, *hidden_parts)

    grad_query = pl.pallas_call(
        second_kernel,
        grid=(blocks, heads),
        in_specs=[vmem_spec, wide_spec, head_spec, head_spec, wide_spec],
        out_specs=wide_spec,
        out_shape=shape((tok_rows, query_width), bf16),
        compiler_params=params,
        cost_estimate=cost(9),
        name="second_pass",
    )(seq_ids, query_rows, key_rows, value_rows, grad_out)

    feats = width // SPAN
    window = -(-feats // 128) * 128
    grad_input_t = pl.pallas_call(
        grad_input_kernel,
        in_specs=[smem_spec, vmem_spec] + [any_spec] * 4,
        out_specs=vmem_spec,
        out_shape=shape((feats, SPAN * tok_rows), bf16),
        scratch_shapes=[
            pltpu.VMEM((SPAN, rank, span), bf16),
            pltpu.VMEM((window, rank), f32),
            pltpu.VMEM((SPAN, feats, rank), bf16),
            pltpu.SemaphoreType.DMA((2,)),
        ],
        compiler_params=params,
        cost_estimate=cost(7),
        name="grad_input",
    )(stores, all_grad, *downs)

    for mask in (1, 2, 4, 8):
        if mask == 4:
            sent, grad_query = together(sent, grad_query)
        if mask == 8:
            sent, down_parts, grad_input_t = together(sent, down_parts, grad_input_t)
        came = swap(sent, mask)
        count = max(came.shape[0] // 2, 1)
        outs = [shape((count,) + came.shape[1:], bf16)]
        if mask < 8:
            outs = [shape(outs[0].shape, f32)] + outs
        halves = pl.pallas_call(
            halve_kernel,
            in_specs=[vmem_spec] * 2,
            out_specs=[vmem_spec] * len(outs),
            out_shape=outs,
            compiler_params=params,
            cost_estimate=cost(1),
            name="halve",
        )(kept, came)
        kept, sent = halves[0], halves[-1]
    grad_up = sent

    grad_down = pl.pallas_call(
        sum_kernel,
        grid=(2 * CHIPS,),
        in_specs=[
            pl.BlockSpec((1, rank, span), lambda p: (p // CHIPS * 8 + p % CHIPS * 2, 0, 0)),
            pl.BlockSpec((1, rank, span), lambda p: (8 - p // CHIPS * 8 + p % CHIPS * 2 + 1, 0, 0)),
        ],
        out_specs=pl.BlockSpec((1, rank, span), lambda p: (0, 0, p)),
        out_shape=shape((1, rank, width), bf16),
        compiler_params=params,
        cost_estimate=cost(2),
        name="sum_down",
    )(down_parts, down_parts)
    return (grad_query, grad_input_t, grad_down, grad_up)


def solution(mesh):
    clustered = mesh.shape["dp"] == SPAN and mesh.shape["groups"] == 2
    in_specs = (
        P(("groups", "dp"), None),
        P(("groups", "dp"), None),
        P(("groups", "dp"), None),
        P(("groups", "dp"), None),
        P(("groups", "dp"), None),
        P("dp", None, None),
        P("dp", None, None),
        P(("groups", "dp")),
        P(),
        P(("groups", "dp"), None),
    )
    out_specs = (
        P(("groups", "dp"), None),
        P("dp", "groups"),
        P(("groups", "dp"), None, None),
        P(("groups", "dp"), None, None),
    )
    return jax.shard_map(
        local_clustered if clustered else local, mesh=mesh, in_specs=in_specs, out_specs=out_specs, check_vma=False
    )
```

```python
import math

import jax
import jax.numpy as jnp
from jax import lax
from jax.experimental import pallas as pl
from jax.experimental.pallas import tpu as pltpu
from jax.sharding import PartitionSpec as P

HD = 128
KVH = 4
GROUP = 8
CHIPS = 4
SPAN = 16


adapter_scale = 2.0
neg_fill = -1e30


def build_mask(seg_ids, block_len):
    position = jnp.arange(seg_ids.shape[0])
    block_ids = position // block_len
    same_block = block_ids[:, None] == block_ids[None, :]
    same_seq = seg_ids[:, None] == seg_ids[None, :]
    causal = position[None, :] <= position[:, None]
    return same_block & same_seq & causal


def first_pass(query_tile, key_tile, grad_tile, keep_mask):
    tile_rows = query_tile.shape[0]
    query_heads = query_tile.reshape(tile_rows, KVH, GROUP, HD)
    key_heads = key_tile.reshape(tile_rows, KVH, HD)
    scores = jnp.einsum(
        "tkgd,skd->kgts", query_heads, key_heads, preferred_element_type=jnp.float32
    ) / math.sqrt(HD)
    scores = jnp.where(keep_mask[None, None], scores, neg_fill)
    attn_probs = jax.nn.softmax(scores, axis=-1)
    probs_b = attn_probs.astype(jnp.bfloat16)
    grad_heads = grad_tile.reshape(tile_rows, KVH, GROUP, HD)
    value_gradient = jnp.einsum(
        "kgts,tkgd->skd", probs_b, grad_heads, preferred_element_type=jnp.float32
    )
    return (attn_probs, probs_b, value_gradient.reshape(tile_rows, KVH * HD).astype(jnp.bfloat16))


def second_pass(attn_probs, probs_b, value_tile, key_tile, grad_tile):
    tile_rows = value_tile.shape[0]
    value_heads = value_tile.reshape(tile_rows, KVH, HD)
    key_heads = key_tile.reshape(tile_rows, KVH, HD)
    grad_heads = grad_tile.reshape(tile_rows, KVH, GROUP, HD)
    out_attn = jnp.einsum(
        "kgts,skd->tkgd", probs_b, value_heads, preferred_element_type=jnp.float32
    )
    dprobs = jnp.einsum(
        "tkgd,skd->kgts", grad_heads, value_heads, preferred_element_type=jnp.float32
    )
    row_delta = jnp.transpose(
        jnp.sum(grad_heads.astype(jnp.float32) * out_attn, axis=-1), (1, 2, 0)
    )[..., None]
    dscores = (attn_probs * (dprobs - row_delta)).astype(jnp.bfloat16)
    grad_heads_q = jnp.einsum(
        "kgts,skd->tkgd", dscores, key_heads, preferred_element_type=jnp.float32
    ) / math.sqrt(HD)
    return grad_heads_q.reshape(tile_rows, KVH * GROUP * HD).astype(jnp.bfloat16)


def local(
    x_rows,
    query_rows,
    key_rows,
    values_base,
    grad_out,
    adapt_down,
    adapt_up,
    block_tenant,
    owner_map,
    seq_ids,
):
    tok_rows = x_rows.shape[0]
    blk_count = block_tenant.shape[0]
    block_len = tok_rows // blk_count
    width = x_rows.shape[1]
    value_width = key_rows.shape[1]
    adapter_count = owner_map.shape[0]
    sliced_down, sliced_up = (
        lax.all_to_all(adapt_down, "dp", split_axis=1, concat_axis=0, tiled=True),
        lax.all_to_all(adapt_up, "dp", split_axis=1, concat_axis=0, tiled=True),
    )
    tenants = lax.all_gather(block_tenant, "dp", axis=0, tiled=True)
    lookup = tenants[:, None] == jnp.arange(adapter_count)[None, :]
    store_rows = jnp.sum(jnp.where(lookup, owner_map[None, :], 0), axis=1)
    picked_down = jnp.take(sliced_down, store_rows, axis=0)
    picked_up = jnp.take(sliced_up, store_rows, axis=0)
    my_down, tenant_up_weight = (
        lax.all_to_all(picked_down, "dp", split_axis=0, concat_axis=1, tiled=True),
        lax.all_to_all(picked_up, "dp", split_axis=0, concat_axis=1, tiled=True),
    )
    tile_rows = min(tok_rows, 512)
    tile_count = tok_rows // tile_rows
    query_tiles = query_rows.reshape(tile_count, tile_rows, -1)
    key_tiles = key_rows.reshape(tile_count, tile_rows, -1)
    grad_tiles = grad_out.reshape(tile_count, tile_rows, -1)
    seq_tiles = seq_ids.reshape(tile_count, tile_rows)
    keep_masks = jax.vmap(lambda ids: build_mask(ids, block_len))(seq_tiles)
    attn_probs, probs_b, value_gradient = jax.vmap(first_pass)(
        query_tiles, key_tiles, grad_tiles, keep_masks
    )
    dvalue_blocks = value_gradient.reshape(blk_count, block_len, value_width)
    x_blocks = x_rows.reshape(blk_count, block_len, width)
    hidden_rows = jnp.einsum(
        "btd,brd->btr", x_blocks, my_down, preferred_element_type=jnp.float32
    ).astype(jnp.bfloat16)
    adapter_values = jnp.einsum(
        "uzd,udv->uzv", hidden_rows, tenant_up_weight, preferred_element_type=jnp.float32
    )
    frozen_value_blocks = values_base.reshape(blk_count, block_len, value_width).astype(jnp.float32)
    value_rows = (frozen_value_blocks + adapter_scale * adapter_values).astype(jnp.bfloat16)
    hidden_gradient = (
        adapter_scale
        * jnp.einsum(
            "bte,bre->btr", dvalue_blocks, tenant_up_weight, preferred_element_type=jnp.float32
        )
    ).astype(jnp.bfloat16)
    part_down = jnp.einsum(
        "btr,btd->brd", hidden_gradient, x_blocks, preferred_element_type=jnp.float32
    )
    partial_up_weight = adapter_scale * jnp.einsum(
        "btr,bte->bre", hidden_rows, dvalue_blocks, preferred_element_type=jnp.float32
    )
    back_down, back_up = (
        lax.all_to_all(part_down, "dp", split_axis=1, concat_axis=0, tiled=True),
        lax.all_to_all(partial_up_weight, "dp", split_axis=1, concat_axis=0, tiled=True),
    )
    selector = (jnp.arange(adapter_count)[:, None] == store_rows[None, :]).astype(jnp.float32)
    sum_down = jnp.einsum("ab,brc->arc", selector, back_down, precision=lax.Precision.HIGHEST)
    sum_up = jnp.einsum("ab,brc->arc", selector, back_up, precision=lax.Precision.HIGHEST)
    grad_down, grad_up = (
        lax.all_to_all(
            sum_down.astype(jnp.bfloat16), "dp", split_axis=0, concat_axis=1, tiled=True
        ),
        lax.all_to_all(sum_up.astype(jnp.bfloat16), "dp", split_axis=0, concat_axis=1, tiled=True),
    )
    local_grad = jnp.einsum(
        "brd,btr->dbt", my_down, hidden_gradient, preferred_element_type=jnp.float32
    )
    local_grad = local_grad.reshape(width, tok_rows).astype(jnp.bfloat16)
    grad_input_t = lax.all_to_all(local_grad, "dp", split_axis=0, concat_axis=1, tiled=True)
    value_tiles = value_rows.reshape(tile_count, tile_rows, value_width)
    grad_query = jax.vmap(second_pass)(attn_probs, probs_b, value_tiles, key_tiles, grad_tiles)
    grad_query = grad_query.reshape(tok_rows, -1)
    return (grad_query, grad_input_t, grad_down, grad_up)


def cost(micros):
    return pl.CostEstimate(flops=0, bytes_accessed=int(micros * 3.3e4), transcendentals=0)


def eighth_of(device):
    return 4 * ((device >> 3) ^ (device & 1)) + ((device >> 1) & 3)


def run_copies(pairs, sems):
    copies = [pltpu.make_async_copy(src, dst, sems.at[k]) for k, (src, dst) in enumerate(pairs)]
    for copy in copies:
        copy.start()
    return copies


def columns(part, span):
    return pl.ds(pl.multiple_of(part * span, 128), span)


def pack_kernel(x_ref, down_ref, down_out, *refs):
    outs, (x_buf, down_buf, sems) = refs[: CHIPS - 1], refs[CHIPS - 1 :]
    me, group = lax.axis_index("dp"), lax.axis_index("groups")
    half, span = down_out.shape[1:]
    ranks = pl.ds(pl.multiple_of(group * half, 16), half)
    pairs = []
    for k in range(CHIPS - 1):
        chip = ((me >> 1) & 3) ^ (k + 1)
        for side in range(2):
            part = 4 * ((me >> 3) ^ side) + chip
            pairs.append((x_ref.at[:, columns(part, span)], x_buf.at[k, :, pl.ds(side * span, span)]))
    pairs.append((down_ref.at[0, ranks, :], down_buf))
    loads = run_copies(pairs, sems)
    pairs = [(x_buf.at[k], outs[k]) for k in range(CHIPS - 1)]
    for dest in range(SPAN):
        pairs.append((down_buf.at[:, pl.ds(eighth_of(dest) * span, span)], down_out.at[dest]))
    stores = [
        pltpu.make_async_copy(src, dst, sems.at[len(loads) + k])
        for k, (src, dst) in enumerate(pairs)
    ]
    for k in range(CHIPS - 1):
        loads[2 * k].wait()
        loads[2 * k + 1].wait()
        stores[k].start()
    loads[-1].wait()
    for copy in stores[CHIPS - 1 :]:
        copy.start()
    for copy in stores:
        copy.wait()


def store_kernel(tenant_ref, owner_ref, slot_ref, row_ref, wide):
    for k in range(2):
        slot_ref[k] = owner_ref[tenant_ref[k]]
    lane = lax.broadcasted_iota(jnp.int32, wide.shape, 1)
    wide[...] = jnp.where(
        lane < wide.shape[1] // 2, slot_ref[0].astype(jnp.float32), slot_ref[1].astype(jnp.float32)
    )
    row_ref[...] = wide[...].astype(jnp.bfloat16)


def heads_in_rows(ref):
    return jnp.concatenate([ref[:, h * HD : (h + 1) * HD] for h in range(GROUP)], axis=0)


def probabilities(ids, keys, queries):
    length = ids.shape[1]
    across = jnp.broadcast_to(ids.astype(jnp.float32), (length, length))
    later = lax.broadcasted_iota(jnp.int32, (length, length), 1)
    earlier = lax.broadcasted_iota(jnp.int32, (length, length), 0)
    keep = (across == across.T) & (earlier <= later)
    scores = lax.dot_general(
        keys, queries, (((1,), (1,)), ((), ())), preferred_element_type=jnp.float32
    ) * (1.0 / math.sqrt(HD))
    scores = jnp.where(jnp.concatenate([keep] * GROUP, axis=1), scores, neg_fill)
    weights = jnp.exp(scores - jnp.max(scores, axis=0, keepdims=True))
    return weights * (1.0 / jnp.sum(weights, axis=0, keepdims=True))


def first_kernel(ids_ref, query_ref, key_ref, grad_ref, dval_ref):
    ids = ids_ref[pl.ds(pl.program_id(0), 1), :]
    probs = probabilities(ids, key_ref[...], heads_in_rows(query_ref)).astype(jnp.bfloat16)
    out = jnp.dot(probs, heads_in_rows(grad_ref), preferred_element_type=jnp.float32)
    dval_ref[...] = out.astype(jnp.bfloat16)


def second_kernel(ids_ref, query_ref, key_ref, value_ref, grad_ref, out_ref):
    ids = ids_ref[pl.ds(pl.program_id(0), 1), :]
    keys = key_ref[...]
    probs = probabilities(ids, keys, heads_in_rows(query_ref))
    dprobs = lax.dot_general(
        value_ref[...],
        heads_in_rows(grad_ref),
        (((1,), (1,)), ((), ())),
        preferred_element_type=jnp.float32,
    )
    rounded = probs.astype(jnp.bfloat16).astype(jnp.float32)
    delta = jnp.sum(rounded * dprobs, axis=0, keepdims=True)
    dscores = (probs * (dprobs - delta)).astype(jnp.bfloat16)
    turned = keys.astype(jnp.float32).T.astype(jnp.bfloat16)
    out = jnp.dot(turned, dscores, preferred_element_type=jnp.float32) * (1.0 / math.sqrt(HD))
    for head in range(GROUP):
        lanes = slice(head * HD, (head + 1) * HD)
        out_ref[:, lanes] = out[:, lanes].T.astype(jnp.bfloat16)


def grad_hidden_kernel(slot_ref, dval_ref, up_ref, *refs):
    out_ref = refs[-1]
    rank = out_ref.shape[0]
    out = lax.dot_general(
        up_ref[0],
        dval_ref[...],
        (((1,), (1,)), ((), ())),
        preferred_element_type=jnp.float32,
    )
    out_ref[...] = (adapter_scale * out).astype(jnp.bfloat16)


def x_copies(x_ref, near, rows):
    me = lax.axis_index("dp")
    chip = (me >> 1) & 3
    span = rows.shape[2] // 2
    pairs = []
    for side in range(2):
        part = 4 * ((me >> 3) ^ side) + chip
        pairs.append((x_ref.at[:, columns(part, span)], rows.at[0, :, pl.ds(side * span, span)]))
    for k, ref in enumerate(near):
        pairs.append((ref, rows.at[k + 1]))
    return pairs


def hidden_kernel(store_ref, x_ref, *refs):
    near, downs, outs, (rows, down, sems) = refs[:3], refs[3:7], refs[7:11], refs[11:]
    me, group = lax.axis_index("dp"), lax.axis_index("groups")
    core = me & 1
    span, half = downs[0].shape[2], downs[0].shape[1]
    block = x_ref.shape[0] // 2
    pairs = x_copies(x_ref, near, rows)
    for slot in range(CHIPS):
        for k in range(2):
            store = store_ref[slot, k]
            for kind, ref in enumerate(downs):
                ranks = pl.ds(pl.multiple_of((group ^ (kind & 1)) * half, 16), half)
                lanes = columns(core ^ (kind >> 1), span)
                pairs.append((ref.at[store], down.at[2 * slot + k, ranks, lanes]))
    for copy in run_copies(pairs, sems):
        copy.wait()
    for slot in range(CHIPS):
        for k in range(2):
            out = lax.dot_general(
                down[2 * slot + k],
                rows[slot, pl.ds(k * block, block), :],
                (((1,), (1,)), ((), ())),
                preferred_element_type=jnp.float32,
            )
            outs[slot][:, pl.ds(k * block, block)] = out


def grad_down_kernel(store_ref, x_ref, *refs):
    grads, near, (keep_ref, send_ref, rows, total, sems) = refs[:4], refs[4:7], refs[8:]
    me = lax.axis_index("dp")
    core = me & 1
    span = keep_ref.shape[2]
    block = x_ref.shape[0] // 2
    copies = run_copies(x_copies(x_ref, near, rows), sems)
    total[...] = jnp.zeros_like(total)
    for copy in copies:
        copy.wait()
    for slot in range(CHIPS):
        for k in range(2):
            store = store_ref[slot, k]
            total[store] += jnp.dot(
                grads[slot][0, :, pl.ds(k * block, block)],
                rows[slot, pl.ds(k * block, block), :],
                preferred_element_type=jnp.float32,
            )
    keep_ref[...] = total[:, :, columns(core, span)].astype(jnp.bfloat16)
    send_ref[...] = total[:, :, columns(1 - core, span)].astype(jnp.bfloat16)


def sum_kernel(part_ref, out_ref):
    span = part_ref.shape[2]
    for part in range(2 * CHIPS):
        one, two = [i for i in range(SPAN) if eighth_of(i) == part]
        out = part_ref[one].astype(jnp.float32) + part_ref[two].astype(jnp.float32)
        out_ref[0, :, pl.ds(part * span, span)] = out.astype(jnp.bfloat16)


def values_kernel(slot_ref, up_slot_ref, base_ref, dval_ref, up_ref, *refs):
    hidden_refs, (val_ref, keep_ref, send_ref) = refs[:CHIPS], refs[CHIPS:]
    rank = keep_ref.shape[1]
    block = base_ref.shape[0] // 2
    hidden = hidden_refs[0][...]
    for ref in hidden_refs[1:]:
        hidden = hidden + ref[...]
    hidden = hidden.astype(jnp.bfloat16)
    keep_ref[...] = jnp.zeros_like(keep_ref)
    send_ref[...] = jnp.zeros_like(send_ref)
    terms = []
    for k in range(2):
        rows = pl.ds(k * block, block)
        part = hidden[:, k * block : (k + 1) * block]
        added = lax.dot_general(
            part,
            up_ref[up_slot_ref[k]],
            (((0,), (0,)), ((), ())),
            preferred_element_type=jnp.float32,
        )
        val_ref[rows, :] = (base_ref[rows, :].astype(jnp.float32) + adapter_scale * added).astype(
            jnp.bfloat16
        )
        terms.append(
            adapter_scale * jnp.dot(part, dval_ref[rows, :], preferred_element_type=jnp.float32)
        )
    same = (slot_ref[0] == slot_ref[1]).astype(jnp.float32)
    terms[1] = terms[1] + same * terms[0]
    for k in range(2):
        for side, ref in enumerate((keep_ref, send_ref)):

            @pl.when((slot_ref[k] & 1) == side)
            def _():
                ref[slot_ref[k] >> 1] = terms[k].astype(ref.dtype)


def halve_kernel(kept_ref, came_ref, *outs):
    for k in range(kept_ref.shape[0]):
        ref = outs[k % len(outs)]
        ref[k // len(outs)] = (kept_ref[k] + came_ref[k].astype(jnp.float32)).astype(ref.dtype)


def grad_input_kernel(store_ref, grad_ref, *refs):
    downs, (out_ref, down, wide, turned, sems) = refs[:4], refs[4:]
    me, group = lax.axis_index("dp"), lax.axis_index("groups")
    core = me & 1
    block = grad_ref.shape[2] // 2
    feats, span = out_ref.shape[0], down.shape[2]
    half = down.shape[1] // 2
    window = wide.shape[0]

    def places(kind):
        ranks = pl.ds(pl.multiple_of((group ^ kind) * half, 16), half)
        return down.at[:, ranks, :]

    for side in range(2):

        @pl.when(core == side)
        def _():
            for kind in range(2):
                src = downs[2 * side + kind]
                pltpu.make_async_copy(src, places(kind), sems.at[kind]).start()

    for kind in range(2):
        pltpu.make_async_copy(downs[kind], places(kind), sems.at[kind]).wait()
    lanes = pl.ds(pl.multiple_of(core * (span - window), 128), window)
    skip = pl.ds(pl.multiple_of(core * (window - feats), 16), feats)
    for store in range(SPAN):
        wide[...] = down[store, :, lanes].astype(jnp.float32).T
        turned[store] = wide[skip, :].astype(jnp.bfloat16)
    for mask in range(SPAN):
        for k in range(2):
            out = jnp.dot(
                turned[store_ref[mask, k]],
                grad_ref[mask, :, pl.ds(k * block, block)],
                preferred_element_type=jnp.float32,
            )
            at = pl.multiple_of(((mask ^ me) * 2 + k) * block, 128)
            out_ref[:, pl.ds(at, block)] = out.astype(jnp.bfloat16)


def together(*values):
    return lax.optimization_barrier(values)


def swap(value, mask):
    return lax.ppermute(value, "dp", [(i, i ^ mask) for i in range(SPAN)])


def spread(value, masks, done=()):
    for mask in masks:
        axis = sum(other > mask for other in done)
        value = jnp.stack([value, swap(value, mask)], axis=axis)
        done = done + (mask,)
    return value


def local_clustered(
    x_rows,
    query_rows,
    key_rows,
    values_base,
    grad_out,
    adapt_down,
    adapt_up,
    block_tenant,
    owner_map,
    seq_ids,
):
    tok_rows, width = x_rows.shape
    value_width = key_rows.shape[1]
    query_width = query_rows.shape[1]
    rank = adapt_down.shape[1]
    blocks, block = seq_ids.shape
    heads = value_width // HD
    span = width // (2 * CHIPS)
    group_width = GROUP * HD
    bf16, f32 = jnp.bfloat16, jnp.float32
    any_spec = pl.BlockSpec(memory_space=pltpu.HBM)
    smem_spec = pl.BlockSpec(memory_space=pltpu.SMEM)
    vmem_spec = pl.BlockSpec(memory_space=pltpu.VMEM)
    shape = jax.ShapeDtypeStruct
    params = pltpu.CompilerParams(vmem_limit_bytes=16 * 1024 * 1024)
    big = pltpu.CompilerParams(vmem_limit_bytes=60 * 1024 * 1024)
    wide_spec = pl.BlockSpec((block, group_width), lambda b, h: (b, h))
    head_spec = pl.BlockSpec((block, HD), lambda b, h: (b, h))

    down_pack, *x_packs = pl.pallas_call(
        pack_kernel,
        in_specs=[any_spec] * 2,
        out_specs=[any_spec] * CHIPS,
        out_shape=[shape((SPAN, rank // 2, span), bf16)]
        + [shape((tok_rows, 2 * span), bf16)] * (CHIPS - 1),
        scratch_shapes=[
            pltpu.VMEM((CHIPS - 1, tok_rows, 2 * span), bf16),
            pltpu.VMEM((rank // 2, width), bf16),
            pltpu.SemaphoreType.DMA((SPAN + 3 * CHIPS,)),
        ],
        compiler_params=big,
        cost_estimate=cost(2.5),
        name="pack",
    )(x_rows, adapt_down)

    slots, slot_rows = pl.pallas_call(
        store_kernel,
        in_specs=[smem_spec] * 2,
        out_specs=[smem_spec, vmem_spec],
        out_shape=[shape((blocks,), jnp.int32), shape((16, value_width), bf16)],
        scratch_shapes=[pltpu.VMEM((16, value_width), f32)],
        compiler_params=params,
        name="store_rows",
    )(block_tenant, owner_map)

    dvalues = pl.pallas_call(
        first_kernel,
        grid=(blocks, heads),
        in_specs=[vmem_spec, wide_spec, head_spec, wide_spec],
        out_specs=head_spec,
        out_shape=shape((tok_rows, value_width), bf16),
        compiler_params=params,
        cost_estimate=cost(7),
        name="first_pass",
    )(seq_ids, query_rows, key_rows, grad_out)

    up_pair = jnp.concatenate([adapt_up[0], swap(adapt_up[0], 8), slot_rows])
    x_packs[0], x_packs[1], x_packs[2], down_pack, up_pair = together(*x_packs, down_pack, up_pair)
    near_up = jnp.stack([up_pair] + [swap(up_pair, 2 * k) for k in range(1, CHIPS)])
    near = [swap(x_packs[k], 2 * (k + 1)) for k in range(CHIPS - 1)]
    down_own = lax.all_to_all(down_pack, "dp", split_axis=0, concat_axis=0, tiled=True)
    near[0], near[1], down_own, near_up, dvalues = together(
        near[0], near[1], down_own, near_up, dvalues
    )
    down_other = lax.ppermute(down_own, "groups", [(0, 1), (1, 0)])
    near_stores = near_up[:, 2 * rank].reshape(CHIPS, 2, -1)[:, :, 0].astype(jnp.int32)
    all_up = jnp.stack([near_up, swap(near_up, 1)])
    stores = jnp.stack([near_stores, swap(near_stores, 1)], axis=1).reshape(2 * CHIPS, blocks)
    stores = jnp.concatenate([stores, swap(stores, 8)])
    all_up = all_up[:, :, : 2 * rank].reshape((SPAN,) + adapt_up.shape[1:])
    me = lax.axis_index("dp")
    slots = slots ^ me
    up_slots = 8 * (slots & 1) + 2 * ((slots >> 1) & 3) + (slots >> 3)

    hidden_gradient = pl.pallas_call(
        grad_hidden_kernel,
        grid_spec=pltpu.PrefetchScalarGridSpec(
            num_scalar_prefetch=1,
            grid=(blocks,),
            in_specs=[
                pl.BlockSpec((block, value_width), lambda b, slot: (b, 0)),
                pl.BlockSpec((1, rank, value_width), lambda b, slot: (slot[b], 0, 0)),
            ],
            out_specs=pl.BlockSpec((rank, block), lambda b, slot: (0, b)),
        ),
        out_shape=shape((rank, tok_rows), bf16),
        compiler_params=params,
        cost_estimate=cost(1),
        name="grad_hidden",
    )(up_slots, dvalues, all_up)
    far_gradient = swap(hidden_gradient, 8)
    hidden_gradient, far_gradient, near[2], near_stores, stores, down_other = together(
        hidden_gradient, far_gradient, near[2], near_stores, stores, down_other
    )
    both = jnp.stack([hidden_gradient, far_gradient])
    near_grad = [both] + [swap(both, 2 * k) for k in range(1, CHIPS)]

    downs = [down_own, down_other, swap(down_own, 1), swap(down_other, 1)]

    hidden_parts = pl.pallas_call(
        hidden_kernel,
        in_specs=[smem_spec] + [any_spec] * (CHIPS + 4),
        out_specs=[vmem_spec] * CHIPS,
        out_shape=[shape((rank, tok_rows), f32)] * CHIPS,
        scratch_shapes=[
            pltpu.VMEM((CHIPS, tok_rows, 2 * span), bf16),
            pltpu.VMEM((2 * CHIPS, rank, 2 * span), bf16),
            pltpu.SemaphoreType.DMA((9 * CHIPS + 1,)),
        ],
        compiler_params=params,
        cost_estimate=cost(3),
        name="hidden",
    )(near_stores, x_rows, *near, *downs)
    own_part = hidden_parts[0]
    hidden_parts = [own_part] + [swap(hidden_parts[k], 2 * k) for k in range(1, CHIPS)]

    down_keep, down_send = pl.pallas_call(
        grad_down_kernel,
        in_specs=[smem_spec, any_spec] + [vmem_spec] * CHIPS + [any_spec] * CHIPS,
        out_specs=[vmem_spec] * 2,
        out_shape=[shape((SPAN, rank, span), bf16)] * 2,
        scratch_shapes=[
            pltpu.VMEM((CHIPS, tok_rows, 2 * span), bf16),
            pltpu.VMEM((SPAN, rank, 2 * span), f32),
            pltpu.SemaphoreType.DMA((CHIPS + 1,)),
        ],
        compiler_params=params,
        cost_estimate=cost(3),
        name="grad_down",
    )(near_stores, x_rows, *near_grad, *near, own_part)
    value_rows, kept, sent = pl.pallas_call(
        values_kernel,
        in_specs=[smem_spec] * 2 + [vmem_spec] * (3 + CHIPS),
        out_specs=[vmem_spec] * 3,
        out_shape=[
            shape((tok_rows, value_width), bf16),
            shape((SPAN // 2, rank, value_width), f32),
            shape((SPAN // 2, rank, value_width), bf16),
        ],
        compiler_params=params,
        cost_estimate=cost(1),
        name="values",
    )(slots, up_slots, values_base, dvalues, all_up, *hidden_parts)

    down_parts = (down_keep.astype(f32) + swap(down_send, 1).astype(f32)).astype(bf16)
    down_parts, value_rows, kept, sent = together(down_parts, value_rows, kept, sent)
    all_grad = jnp.stack(near_grad, axis=1)
    all_grad = jnp.stack([all_grad, swap(all_grad, 1)], axis=2)
    all_grad = all_grad.reshape((SPAN,) + hidden_gradient.shape)
    down_parts = lax.all_to_all(down_parts, "dp", split_axis=0, concat_axis=0, tiled=True)


    grad_query = pl.pallas_call(
        second_kernel,
        grid=(blocks, heads),
        in_specs=[vmem_spec, wide_spec, head_spec, head_spec, wide_spec],
        out_specs=wide_spec,
        out_shape=shape((tok_rows, query_width), bf16),
        compiler_params=params,
        cost_estimate=cost(9),
        name="second_pass",
    )(seq_ids, query_rows, key_rows, value_rows, grad_out)

    feats = width // SPAN
    window = -(-feats // 128) * 128
    grad_input_t = pl.pallas_call(
        grad_input_kernel,
        in_specs=[smem_spec, vmem_spec] + [any_spec] * 4,
        out_specs=vmem_spec,
        out_shape=shape((feats, SPAN * tok_rows), bf16),
        scratch_shapes=[
            pltpu.VMEM((SPAN, rank, span), bf16),
            pltpu.VMEM((window, rank), f32),
            pltpu.VMEM((SPAN, feats, rank), bf16),
            pltpu.SemaphoreType.DMA((2,)),
        ],
        compiler_params=params,
        cost_estimate=cost(7),
        name="grad_input",
    )(stores, all_grad, *downs)

    for mask in (1, 2, 4, 8):
        if mask == 4:
            sent, grad_query = together(sent, grad_query)
        if mask == 8:
            sent, down_parts, grad_input_t = together(sent, down_parts, grad_input_t)
        came = swap(sent, mask)
        count = max(came.shape[0] // 2, 1)
        outs = [shape((count,) + came.shape[1:], bf16)]
        if mask < 8:
            outs = [shape(outs[0].shape, f32)] + outs
        halves = pl.pallas_call(
            halve_kernel,
            in_specs=[vmem_spec] * 2,
            out_specs=[vmem_spec] * len(outs),
            out_shape=outs,
            compiler_params=params,
            cost_estimate=cost(1),
            name="halve",
        )(kept, came)
        kept, sent = halves[0], halves[-1]
    grad_up = sent

    grad_down = pl.pallas_call(
        sum_kernel,
        in_specs=[vmem_spec],
        out_specs=vmem_spec,
        out_shape=shape((1, rank, width), bf16),
        compiler_params=params,
        cost_estimate=cost(2),
        name="sum_down",
    )(down_parts)
    return (grad_query, grad_input_t, grad_down, grad_up)


def solution(mesh):
    clustered = mesh.shape["dp"] == SPAN and mesh.shape["groups"] == 2
    in_specs = (
        P(("groups", "dp"), None),
        P(("groups", "dp"), None),
        P(("groups", "dp"), None),
        P(("groups", "dp"), None),
        P(("groups", "dp"), None),
        P("dp", None, None),
        P("dp", None, None),
        P(("groups", "dp")),
        P(),
        P(("groups", "dp"), None),
    )
    out_specs = (
        P(("groups", "dp"), None),
        P("dp", "groups"),
        P(("groups", "dp"), None, None),
        P(("groups", "dp"), None, None),
    )
    return jax.shard_map(
        local_clustered if clustered else local, mesh=mesh, in_specs=in_specs, out_specs=out_specs, check_vma=False
    )
```

```python
import functools
import math

import jax
import jax.numpy as jnp
from jax import lax
from jax.experimental import pallas as pl
from jax.experimental.pallas import tpu as pltpu
from jax.sharding import PartitionSpec as P

HD = 128
KVH = 4
GROUP = 8
CHIPS = 4
SPAN = 16


adapter_scale = 2.0
neg_fill = -1e30


def build_mask(seg_ids, block_len):
    position = jnp.arange(seg_ids.shape[0])
    block_ids = position // block_len
    same_block = block_ids[:, None] == block_ids[None, :]
    same_seq = seg_ids[:, None] == seg_ids[None, :]
    causal = position[None, :] <= position[:, None]
    return same_block & same_seq & causal


def first_pass(query_tile, key_tile, grad_tile, keep_mask):
    tile_rows = query_tile.shape[0]
    query_heads = query_tile.reshape(tile_rows, KVH, GROUP, HD)
    key_heads = key_tile.reshape(tile_rows, KVH, HD)
    scores = jnp.einsum(
        "tkgd,skd->kgts", query_heads, key_heads, preferred_element_type=jnp.float32
    ) / math.sqrt(HD)
    scores = jnp.where(keep_mask[None, None], scores, neg_fill)
    attn_probs = jax.nn.softmax(scores, axis=-1)
    probs_b = attn_probs.astype(jnp.bfloat16)
    grad_heads = grad_tile.reshape(tile_rows, KVH, GROUP, HD)
    value_gradient = jnp.einsum(
        "kgts,tkgd->skd", probs_b, grad_heads, preferred_element_type=jnp.float32
    )
    return (attn_probs, probs_b, value_gradient.reshape(tile_rows, KVH * HD).astype(jnp.bfloat16))


def second_pass(attn_probs, probs_b, value_tile, key_tile, grad_tile):
    tile_rows = value_tile.shape[0]
    value_heads = value_tile.reshape(tile_rows, KVH, HD)
    key_heads = key_tile.reshape(tile_rows, KVH, HD)
    grad_heads = grad_tile.reshape(tile_rows, KVH, GROUP, HD)
    out_attn = jnp.einsum(
        "kgts,skd->tkgd", probs_b, value_heads, preferred_element_type=jnp.float32
    )
    dprobs = jnp.einsum(
        "tkgd,skd->kgts", grad_heads, value_heads, preferred_element_type=jnp.float32
    )
    row_delta = jnp.transpose(
        jnp.sum(grad_heads.astype(jnp.float32) * out_attn, axis=-1), (1, 2, 0)
    )[..., None]
    dscores = (attn_probs * (dprobs - row_delta)).astype(jnp.bfloat16)
    grad_heads_q = jnp.einsum(
        "kgts,skd->tkgd", dscores, key_heads, preferred_element_type=jnp.float32
    ) / math.sqrt(HD)
    return grad_heads_q.reshape(tile_rows, KVH * GROUP * HD).astype(jnp.bfloat16)


def local(
    x_rows,
    query_rows,
    key_rows,
    values_base,
    grad_out,
    adapt_down,
    adapt_up,
    block_tenant,
    owner_map,
    seq_ids,
):
    tok_rows = x_rows.shape[0]
    blk_count = block_tenant.shape[0]
    block_len = tok_rows // blk_count
    width = x_rows.shape[1]
    value_width = key_rows.shape[1]
    adapter_count = owner_map.shape[0]
    sliced_down, sliced_up = (
        lax.all_to_all(adapt_down, "dp", split_axis=1, concat_axis=0, tiled=True),
        lax.all_to_all(adapt_up, "dp", split_axis=1, concat_axis=0, tiled=True),
    )
    tenants = lax.all_gather(block_tenant, "dp", axis=0, tiled=True)
    lookup = tenants[:, None] == jnp.arange(adapter_count)[None, :]
    store_rows = jnp.sum(jnp.where(lookup, owner_map[None, :], 0), axis=1)
    picked_down = jnp.take(sliced_down, store_rows, axis=0)
    picked_up = jnp.take(sliced_up, store_rows, axis=0)
    my_down, tenant_up_weight = (
        lax.all_to_all(picked_down, "dp", split_axis=0, concat_axis=1, tiled=True),
        lax.all_to_all(picked_up, "dp", split_axis=0, concat_axis=1, tiled=True),
    )
    tile_rows = min(tok_rows, 512)
    tile_count = tok_rows // tile_rows
    query_tiles = query_rows.reshape(tile_count, tile_rows, -1)
    key_tiles = key_rows.reshape(tile_count, tile_rows, -1)
    grad_tiles = grad_out.reshape(tile_count, tile_rows, -1)
    seq_tiles = seq_ids.reshape(tile_count, tile_rows)
    keep_masks = jax.vmap(lambda ids: build_mask(ids, block_len))(seq_tiles)
    attn_probs, probs_b, value_gradient = jax.vmap(first_pass)(
        query_tiles, key_tiles, grad_tiles, keep_masks
    )
    dvalue_blocks = value_gradient.reshape(blk_count, block_len, value_width)
    x_blocks = x_rows.reshape(blk_count, block_len, width)
    hidden_rows = jnp.einsum(
        "btd,brd->btr", x_blocks, my_down, preferred_element_type=jnp.float32
    ).astype(jnp.bfloat16)
    adapter_values = jnp.einsum(
        "uzd,udv->uzv", hidden_rows, tenant_up_weight, preferred_element_type=jnp.float32
    )
    frozen_value_blocks = values_base.reshape(blk_count, block_len, value_width).astype(jnp.float32)
    value_rows = (frozen_value_blocks + adapter_scale * adapter_values).astype(jnp.bfloat16)
    hidden_gradient = (
        adapter_scale
        * jnp.einsum(
            "bte,bre->btr", dvalue_blocks, tenant_up_weight, preferred_element_type=jnp.float32
        )
    ).astype(jnp.bfloat16)
    part_down = jnp.einsum(
        "btr,btd->brd", hidden_gradient, x_blocks, preferred_element_type=jnp.float32
    )
    partial_up_weight = adapter_scale * jnp.einsum(
        "btr,bte->bre", hidden_rows, dvalue_blocks, preferred_element_type=jnp.float32
    )
    back_down, back_up = (
        lax.all_to_all(part_down, "dp", split_axis=1, concat_axis=0, tiled=True),
        lax.all_to_all(partial_up_weight, "dp", split_axis=1, concat_axis=0, tiled=True),
    )
    selector = (jnp.arange(adapter_count)[:, None] == store_rows[None, :]).astype(jnp.float32)
    sum_down = jnp.einsum("ab,brc->arc", selector, back_down, precision=lax.Precision.HIGHEST)
    sum_up = jnp.einsum("ab,brc->arc", selector, back_up, precision=lax.Precision.HIGHEST)
    grad_down, grad_up = (
        lax.all_to_all(
            sum_down.astype(jnp.bfloat16), "dp", split_axis=0, concat_axis=1, tiled=True
        ),
        lax.all_to_all(sum_up.astype(jnp.bfloat16), "dp", split_axis=0, concat_axis=1, tiled=True),
    )
    local_grad = jnp.einsum(
        "brd,btr->dbt", my_down, hidden_gradient, preferred_element_type=jnp.float32
    )
    local_grad = local_grad.reshape(width, tok_rows).astype(jnp.bfloat16)
    grad_input_t = lax.all_to_all(local_grad, "dp", split_axis=0, concat_axis=1, tiled=True)
    value_tiles = value_rows.reshape(tile_count, tile_rows, value_width)
    grad_query = jax.vmap(second_pass)(attn_probs, probs_b, value_tiles, key_tiles, grad_tiles)
    grad_query = grad_query.reshape(tok_rows, -1)
    return (grad_query, grad_input_t, grad_down, grad_up)


def cost(micros):
    return pl.CostEstimate(flops=0, bytes_accessed=int(micros * 3.3e4), transcendentals=0)


def eighth_of(device):
    return 4 * ((device >> 3) ^ (device & 1)) + ((device >> 1) & 3)


def run_copies(pairs, sems):
    copies = [pltpu.make_async_copy(src, dst, sems.at[k]) for k, (src, dst) in enumerate(pairs)]
    for copy in copies:
        copy.start()
    return copies


def columns(part, span):
    return pl.ds(pl.multiple_of(part * span, 128), span)


def pack_kernel(x_ref, down_ref, down_out, *refs):
    outs, (x_buf, down_buf, sems) = refs[: CHIPS - 1], refs[CHIPS - 1 :]
    me, group = lax.axis_index("dp"), lax.axis_index("groups")
    half, span = down_out.shape[1:]
    ranks = pl.ds(pl.multiple_of(group * half, 16), half)
    pairs = []
    for k in range(CHIPS - 1):
        chip = ((me >> 1) & 3) ^ (k + 1)
        for side in range(2):
            part = 4 * ((me >> 3) ^ side) + chip
            pairs.append((x_ref.at[:, columns(part, span)], x_buf.at[k, :, pl.ds(side * span, span)]))
    pairs.append((down_ref.at[0, ranks, :], down_buf))
    loads = run_copies(pairs, sems)
    pairs = [(x_buf.at[k], outs[k]) for k in range(CHIPS - 1)]
    for dest in range(SPAN):
        pairs.append((down_buf.at[:, pl.ds(eighth_of(dest) * span, span)], down_out.at[dest]))
    stores = [
        pltpu.make_async_copy(src, dst, sems.at[len(loads) + k])
        for k, (src, dst) in enumerate(pairs)
    ]
    for k in range(CHIPS - 1):
        loads[2 * k].wait()
        loads[2 * k + 1].wait()
        stores[k].start()
    loads[-1].wait()
    for copy in stores[CHIPS - 1 :]:
        copy.start()
    for copy in stores:
        copy.wait()


def store_kernel(tenant_ref, owner_ref, out_ref):
    for k in range(2):
        out_ref[k] = owner_ref[tenant_ref[k]]


def heads_in_rows(ref):
    return jnp.concatenate([ref[:, h * HD : (h + 1) * HD] for h in range(GROUP)], axis=0)


def probabilities(ids, keys, queries):
    length = ids.shape[1]
    across = jnp.broadcast_to(ids.astype(jnp.float32), (length, length))
    later = lax.broadcasted_iota(jnp.int32, (length, length), 1)
    earlier = lax.broadcasted_iota(jnp.int32, (length, length), 0)
    keep = (across == across.T) & (earlier <= later)
    scores = lax.dot_general(
        keys, queries, (((1,), (1,)), ((), ())), preferred_element_type=jnp.float32
    ) * (1.0 / math.sqrt(HD))
    scores = jnp.where(jnp.concatenate([keep] * GROUP, axis=1), scores, neg_fill)
    weights = jnp.exp(scores - jnp.max(scores, axis=0, keepdims=True))
    return weights * (1.0 / jnp.sum(weights, axis=0, keepdims=True))


def first_kernel(ids_ref, query_ref, key_ref, grad_ref, dval_ref):
    ids = ids_ref[pl.ds(pl.program_id(0), 1), :]
    probs = probabilities(ids, key_ref[...], heads_in_rows(query_ref)).astype(jnp.bfloat16)
    out = jnp.dot(probs, heads_in_rows(grad_ref), preferred_element_type=jnp.float32)
    dval_ref[...] = out.astype(jnp.bfloat16)


def second_kernel(ids_ref, query_ref, key_ref, value_ref, grad_ref, out_ref):
    ids = ids_ref[pl.ds(pl.program_id(0), 1), :]
    keys = key_ref[...]
    probs = probabilities(ids, keys, heads_in_rows(query_ref))
    dprobs = lax.dot_general(
        value_ref[...],
        heads_in_rows(grad_ref),
        (((1,), (1,)), ((), ())),
        preferred_element_type=jnp.float32,
    )
    rounded = probs.astype(jnp.bfloat16).astype(jnp.float32)
    delta = jnp.sum(rounded * dprobs, axis=0, keepdims=True)
    dscores = (probs * (dprobs - delta)).astype(jnp.bfloat16)
    turned = keys.astype(jnp.float32).T.astype(jnp.bfloat16)
    out = jnp.dot(turned, dscores, preferred_element_type=jnp.float32) * (1.0 / math.sqrt(HD))
    for head in range(GROUP):
        lanes = slice(head * HD, (head + 1) * HD)
        out_ref[:, lanes] = out[:, lanes].T.astype(jnp.bfloat16)


def grad_hidden_kernel(slot_ref, store_ref, dval_ref, up_ref, out_ref):
    rank = up_ref.shape[1]
    out = lax.dot_general(
        up_ref[0], dval_ref[...], (((1,), (1,)), ((), ())), preferred_element_type=jnp.float32
    )
    out_ref[pl.ds(0, rank), :] = (adapter_scale * out).astype(jnp.bfloat16)
    store = store_ref[pl.program_id(0)].astype(jnp.float32)
    below = jnp.full((16, out_ref.shape[1]), store, jnp.float32)
    out_ref[pl.ds(rank, 16), :] = below.astype(jnp.bfloat16)


def read_stores(values, rank, wide, stores, sem):
    for k, value in enumerate(values):
        row = value[pl.ds(rank, 16), :].astype(jnp.float32)[0:1, :]
        wide[pl.ds(k, 1), :] = row.astype(jnp.int32)
    copy = pltpu.make_async_copy(wide, stores, sem)
    copy.start()
    copy.wait()


def x_copies(x_ref, near, rows):
    me = lax.axis_index("dp")
    chip = (me >> 1) & 3
    span = rows.shape[2] // 2
    pairs = []
    for side in range(2):
        part = 4 * ((me >> 3) ^ side) + chip
        pairs.append((x_ref.at[:, columns(part, span)], rows.at[0, :, pl.ds(side * span, span)]))
    for k, ref in enumerate(near):
        pairs.append((ref, rows.at[k + 1]))
    return pairs


def hidden_kernel(x_ref, *refs):
    grads, near, downs, outs = refs[:4], refs[4:7], refs[7:11], refs[11:15]
    rows, down, wide, stores, sems = refs[15:]
    me, group = lax.axis_index("dp"), lax.axis_index("groups")
    core = me & 1
    span, half = downs[0].shape[2], downs[0].shape[1]
    block = x_ref.shape[0] // 2
    copies = run_copies(x_copies(x_ref, near, rows), sems)
    read_stores(grads, 2 * half, wide, stores, sems.at[len(copies)])
    for slot in range(CHIPS):
        for k in range(2):
            store = stores[slot, k * block]
            for kind, ref in enumerate(downs):
                ranks = pl.ds(pl.multiple_of((group ^ (kind & 1)) * half, 16), half)
                lanes = columns(core ^ (kind >> 1), span)
                copy = pltpu.make_async_copy(
                    ref.at[store], down.at[2 * slot + k, ranks, lanes], sems.at[len(copies) + 1]
                )
                copy.start()
                copies.append(copy)
    for copy in copies:
        copy.wait()
    for slot in range(CHIPS):
        for k in range(2):
            out = lax.dot_general(
                down[2 * slot + k],
                rows[slot, pl.ds(k * block, block), :],
                (((1,), (1,)), ((), ())),
                preferred_element_type=jnp.float32,
            )
            outs[slot][:, pl.ds(k * block, block)] = out


def grad_down_kernel(x_ref, *refs):
    grads, near, (keep_ref, send_ref, rows, total, wide, stores, sems) = refs[:4], refs[4:7], refs[7:]
    core = lax.axis_index("dp") & 1
    rank, span = keep_ref.shape[1:]
    block = x_ref.shape[0] // 2
    copies = run_copies(x_copies(x_ref, near, rows), sems)
    read_stores(grads, rank, wide, stores, sems.at[len(copies)])
    total[...] = jnp.zeros_like(total)
    for copy in copies:
        copy.wait()
    for slot in range(CHIPS):
        for k in range(2):
            total[stores[slot, k * block]] += jnp.dot(
                grads[slot][pl.ds(0, rank), pl.ds(k * block, block)],
                rows[slot, pl.ds(k * block, block), :],
                preferred_element_type=jnp.float32,
            )
    keep_ref[...] = total[:, :, columns(core, span)].astype(jnp.bfloat16)
    send_ref[...] = total[:, :, columns(1 - core, span)].astype(jnp.bfloat16)


def sum_kernel(part_ref, out_ref):
    span = part_ref.shape[2]
    for part in range(2 * CHIPS):
        one, two = [i for i in range(SPAN) if eighth_of(i) == part]
        out = part_ref[one].astype(jnp.float32) + part_ref[two].astype(jnp.float32)
        out_ref[0, :, pl.ds(part * span, span)] = out.astype(jnp.bfloat16)


def values_kernel(slot_ref, up_slot_ref, base_ref, dval_ref, up_ref, *refs):
    hidden_refs, (val_ref, keep_ref, send_ref) = refs[:CHIPS], refs[CHIPS + 1 :]
    rank = keep_ref.shape[1]
    block = base_ref.shape[0] // 2
    hidden = hidden_refs[0][...]
    for ref in hidden_refs[1:]:
        hidden = hidden + ref[...]
    hidden = hidden.astype(jnp.bfloat16)
    keep_ref[...] = jnp.zeros_like(keep_ref)
    send_ref[...] = jnp.zeros_like(send_ref)
    terms = []
    for k in range(2):
        rows = pl.ds(k * block, block)
        part = hidden[:, k * block : (k + 1) * block]
        added = lax.dot_general(
            part,
            up_ref[up_slot_ref[k]],
            (((0,), (0,)), ((), ())),
            preferred_element_type=jnp.float32,
        )
        val_ref[rows, :] = (base_ref[rows, :].astype(jnp.float32) + adapter_scale * added).astype(
            jnp.bfloat16
        )
        terms.append(
            adapter_scale * jnp.dot(part, dval_ref[rows, :], preferred_element_type=jnp.float32)
        )
    same = (slot_ref[0] == slot_ref[1]).astype(jnp.float32)
    terms[1] = terms[1] + same * terms[0]
    for k in range(2):
        for side, ref in enumerate((keep_ref, send_ref)):

            @pl.when((slot_ref[k] & 1) == side)
            def _():
                ref[slot_ref[k] >> 1] = terms[k].astype(ref.dtype)


def halve_kernel(kept_ref, came_ref, *outs, extra=0):
    outs = outs[extra:]
    for k in range(kept_ref.shape[0]):
        ref = outs[k % len(outs)]
        ref[k // len(outs)] = (kept_ref[k] + came_ref[k].astype(jnp.float32)).astype(ref.dtype)


def grad_input_kernel(grad_ref, *refs):
    downs, (out_ref, down, wide, turned, marks, stores, sems) = refs[:4], refs[4:]
    me, group = lax.axis_index("dp"), lax.axis_index("groups")
    core = me & 1
    block = grad_ref.shape[2] // 2
    feats, span = out_ref.shape[0], down.shape[2]
    half = down.shape[1] // 2
    window = wide.shape[0]

    def places(kind):
        ranks = pl.ds(pl.multiple_of((group ^ kind) * half, 16), half)
        return down.at[:, ranks, :]

    for side in range(2):

        @pl.when(core == side)
        def _():
            for kind in range(2):
                src = downs[2 * side + kind]
                pltpu.make_async_copy(src, places(kind), sems.at[kind]).start()

    read_stores([grad_ref.at[k] for k in range(SPAN)], 2 * half, marks, stores, sems.at[2])
    for kind in range(2):
        pltpu.make_async_copy(downs[kind], places(kind), sems.at[kind]).wait()
    lanes = pl.ds(pl.multiple_of(core * (span - window), 128), window)
    skip = pl.ds(pl.multiple_of(core * (window - feats), 16), feats)
    for store in range(SPAN):
        wide[...] = down[store, :, lanes].astype(jnp.float32).T
        turned[store] = wide[skip, :].astype(jnp.bfloat16)
    for mask in range(SPAN):
        for k in range(2):
            out = jnp.dot(
                turned[stores[mask, k * block]],
                grad_ref[mask, pl.ds(0, 2 * half), pl.ds(k * block, block)],
                preferred_element_type=jnp.float32,
            )
            at = pl.multiple_of(((mask ^ me) * 2 + k) * block, 128)
            out_ref[:, pl.ds(at, block)] = out.astype(jnp.bfloat16)


def together(*values):
    return lax.optimization_barrier(values)


def swap(value, mask):
    return lax.ppermute(value, "dp", [(i, i ^ mask) for i in range(SPAN)])


def spread(value, masks, done=()):
    for mask in masks:
        axis = sum(other > mask for other in done)
        value = jnp.stack([value, swap(value, mask)], axis=axis)
        done = done + (mask,)
    return value


def local_clustered(
    x_rows,
    query_rows,
    key_rows,
    values_base,
    grad_out,
    adapt_down,
    adapt_up,
    block_tenant,
    owner_map,
    seq_ids,
):
    tok_rows, width = x_rows.shape
    value_width = key_rows.shape[1]
    query_width = query_rows.shape[1]
    rank = adapt_down.shape[1]
    blocks, block = seq_ids.shape
    heads = value_width // HD
    span = width // (2 * CHIPS)
    group_width = GROUP * HD
    bf16, f32 = jnp.bfloat16, jnp.float32
    any_spec = pl.BlockSpec(memory_space=pltpu.HBM)
    smem_spec = pl.BlockSpec(memory_space=pltpu.SMEM)
    vmem_spec = pl.BlockSpec(memory_space=pltpu.VMEM)
    shape = jax.ShapeDtypeStruct
    params = pltpu.CompilerParams(vmem_limit_bytes=16 * 1024 * 1024)
    big = pltpu.CompilerParams(vmem_limit_bytes=60 * 1024 * 1024)
    wide_spec = pl.BlockSpec((block, group_width), lambda b, h: (b, h))
    head_spec = pl.BlockSpec((block, HD), lambda b, h: (b, h))

    down_pack, *x_packs = pl.pallas_call(
        pack_kernel,
        in_specs=[any_spec] * 2,
        out_specs=[any_spec] * CHIPS,
        out_shape=[shape((SPAN, rank // 2, span), bf16)]
        + [shape((tok_rows, 2 * span), bf16)] * (CHIPS - 1),
        scratch_shapes=[
            pltpu.VMEM((CHIPS - 1, tok_rows, 2 * span), bf16),
            pltpu.VMEM((rank // 2, width), bf16),
            pltpu.SemaphoreType.DMA((SPAN + 3 * CHIPS,)),
        ],
        compiler_params=big,
        cost_estimate=cost(2.5),
        name="pack",
    )(x_rows, adapt_down)

    own_stores = pl.pallas_call(
        store_kernel,
        in_specs=[smem_spec] * 2,
        out_specs=smem_spec,
        out_shape=shape((blocks,), jnp.int32),
        name="store_rows",
    )(block_tenant, owner_map)

    dvalues = pl.pallas_call(
        first_kernel,
        grid=(blocks, heads),
        in_specs=[vmem_spec, wide_spec, head_spec, wide_spec],
        out_specs=head_spec,
        out_shape=shape((tok_rows, value_width), bf16),
        compiler_params=params,
        cost_estimate=cost(7),
        name="first_pass",
    )(seq_ids, query_rows, key_rows, grad_out)

    up_pair = jnp.concatenate([adapt_up, swap(adapt_up, 8)])
    x_packs[0], x_packs[1], x_packs[2], up_pair = together(*x_packs, up_pair)
    peers = [[first + 2 * k for k in range(CHIPS)] for first in (0, 1, 8, 9)]
    near_up = lax.all_to_all(
        jnp.broadcast_to(up_pair, (CHIPS,) + up_pair.shape), "dp", 0, 0, axis_index_groups=peers
    )
    near = [swap(x_packs[k], 2 * (k + 1)) for k in range(CHIPS - 1)]
    down_pack, near_up = together(down_pack, near_up)
    down_own = lax.all_to_all(down_pack, "dp", split_axis=0, concat_axis=0, tiled=True)
    near[0], near[1], near_up, dvalues = together(near[0], near[1], near_up, dvalues)
    all_up = jnp.stack([near_up, swap(near_up, 1)]).reshape((SPAN,) + adapt_up.shape[1:])
    me = lax.axis_index("dp")
    slots = own_stores ^ me
    up_slots = 8 * (slots & 1) + (own_stores & 6) + (slots >> 3)

    hidden_gradient = pl.pallas_call(
        grad_hidden_kernel,
        grid_spec=pltpu.PrefetchScalarGridSpec(
            num_scalar_prefetch=2,
            grid=(blocks,),
            in_specs=[
                pl.BlockSpec((block, value_width), lambda b, slot, store: (b, 0)),
                pl.BlockSpec((1, rank, value_width), lambda b, slot, store: (slot[b], 0, 0)),
            ],
            out_specs=pl.BlockSpec((rank + 16, block), lambda b, slot, store: (0, b)),
        ),
        out_shape=shape((rank + 16, tok_rows), bf16),
        compiler_params=params,
        cost_estimate=cost(1),
        name="grad_hidden",
    )(up_slots, own_stores, dvalues, all_up)
    down_own, hidden_gradient = together(down_own, hidden_gradient)
    near_grad = [hidden_gradient] + [swap(hidden_gradient, 2 * k) for k in range(1, CHIPS)]
    down_other = lax.ppermute(down_own, "groups", [(0, 1), (1, 0)])
    down_other, *held = together(down_other, near[2], *near_grad)
    downs = [down_own, down_other, swap(down_own, 1), swap(down_other, 1)]

    hidden_parts = pl.pallas_call(
        hidden_kernel,
        in_specs=[any_spec] + [vmem_spec] * CHIPS + [any_spec] * (CHIPS + 3),
        out_specs=[vmem_spec] * CHIPS,
        out_shape=[shape((rank, tok_rows), f32)] * CHIPS,
        scratch_shapes=[
            pltpu.VMEM((CHIPS, tok_rows, 2 * span), bf16),
            pltpu.VMEM((2 * CHIPS, rank, 2 * span), bf16),
            pltpu.VMEM((8, tok_rows), jnp.int32),
            pltpu.SMEM((8, tok_rows), jnp.int32),
            pltpu.SemaphoreType.DMA((9 * CHIPS + 2,)),
        ],
        compiler_params=params,
        cost_estimate=cost(3),
        name="hidden",
    )(x_rows, *held[1:], near[0], near[1], held[0], *downs)
    own_part = hidden_parts[0]
    hidden_parts = [swap(hidden_parts[k], 2 * k) for k in range(1, CHIPS)]

    down_keep, down_send = pl.pallas_call(
        grad_down_kernel,
        in_specs=[any_spec] + [vmem_spec] * CHIPS + [any_spec] * (CHIPS - 1),
        out_specs=[vmem_spec] * 2,
        out_shape=[shape((SPAN, rank, span), bf16)] * 2,
        scratch_shapes=[
            pltpu.VMEM((CHIPS, tok_rows, 2 * span), bf16),
            pltpu.VMEM((SPAN, rank, 2 * span), f32),
            pltpu.VMEM((8, tok_rows), jnp.int32),
            pltpu.SMEM((8, tok_rows), jnp.int32),
            pltpu.SemaphoreType.DMA((CHIPS + 2,)),
        ],
        compiler_params=params,
        cost_estimate=cost(3),
        name="grad_down",
    )(x_rows, *near_grad, *near)
    all_grad = jnp.stack(near_grad)
    far_grad, own_part = together(swap(all_grad, 8), own_part)
    all_grad = jnp.stack([all_grad, far_grad])
    down_parts = (down_keep.astype(f32) + swap(down_send, 1).astype(f32)).astype(bf16)
    value_rows, kept, sent = pl.pallas_call(
        values_kernel,
        in_specs=[smem_spec] * 2 + [vmem_spec] * (3 + CHIPS) + [any_spec],
        out_specs=[vmem_spec] * 3,
        out_shape=[
            shape((tok_rows, value_width), bf16),
            shape((SPAN // 2, rank, value_width), f32),
            shape((SPAN // 2, rank, value_width), bf16),
        ],
        compiler_params=params,
        cost_estimate=cost(1),
        name="values",
    )(slots, up_slots, values_base, dvalues, all_up, own_part, *hidden_parts, down_parts)

    down_parts, value_rows, kept, sent, all_grad = together(
        down_parts, value_rows, kept, sent, all_grad
    )
    all_grad = jnp.stack([all_grad, swap(all_grad, 1)], axis=2)
    all_grad = all_grad.reshape((SPAN,) + hidden_gradient.shape)
    down_parts = lax.all_to_all(down_parts, "dp", split_axis=0, concat_axis=0, tiled=True)


    grad_query = pl.pallas_call(
        second_kernel,
        grid=(blocks, heads),
        in_specs=[vmem_spec, wide_spec, head_spec, head_spec, wide_spec],
        out_specs=wide_spec,
        out_shape=shape((tok_rows, query_width), bf16),
        compiler_params=params,
        cost_estimate=cost(9),
        name="second_pass",
    )(seq_ids, query_rows, key_rows, value_rows, grad_out)

    feats = width // SPAN
    window = -(-feats // 128) * 128
    grad_input_t = pl.pallas_call(
        grad_input_kernel,
        in_specs=[vmem_spec] + [any_spec] * 4,
        out_specs=vmem_spec,
        out_shape=shape((feats, SPAN * tok_rows), bf16),
        scratch_shapes=[
            pltpu.VMEM((SPAN, rank, span), bf16),
            pltpu.VMEM((window, rank), f32),
            pltpu.VMEM((SPAN, feats, rank), bf16),
            pltpu.VMEM((SPAN, tok_rows), jnp.int32),
            pltpu.SMEM((SPAN, tok_rows), jnp.int32),
            pltpu.SemaphoreType.DMA((3,)),
        ],
        compiler_params=params,
        cost_estimate=cost(7),
        name="grad_input",
    )(all_grad, *downs)

    grad_down = pl.pallas_call(
        sum_kernel,
        in_specs=[vmem_spec],
        out_specs=vmem_spec,
        out_shape=shape((1, rank, width), bf16),
        compiler_params=params,
        cost_estimate=cost(2),
        name="sum_down",
    )(down_parts)
    for mask in (1, 2, 4, 8):
        if mask == 4:
            sent, grad_query = together(sent, grad_query)
        if mask == 8:
            sent, grad_input_t = together(sent, grad_input_t)
        came = swap(sent, mask)
        last = (grad_down,) if mask == 8 else ()
        count = max(came.shape[0] // 2, 1)
        outs = [shape((count,) + came.shape[1:], bf16)]
        if mask < 8:
            outs = [shape(outs[0].shape, f32)] + outs
        halves = pl.pallas_call(
            functools.partial(halve_kernel, extra=len(last)),
            in_specs=[vmem_spec] * 2 + [any_spec] * len(last),
            out_specs=[vmem_spec] * len(outs),
            out_shape=outs,
            compiler_params=params,
            cost_estimate=cost(1),
            name="halve",
        )(kept, came, *last)
        kept, sent = halves[0], halves[-1]
    grad_up = sent

    return (grad_query, grad_input_t, grad_down, grad_up)


def solution(mesh):
    clustered = mesh.shape["dp"] == SPAN and mesh.shape["groups"] == 2
    in_specs = (
        P(("groups", "dp"), None),
        P(("groups", "dp"), None),
        P(("groups", "dp"), None),
        P(("groups", "dp"), None),
        P(("groups", "dp"), None),
        P("dp", None, None),
        P("dp", None, None),
        P(("groups", "dp")),
        P(),
        P(("groups", "dp"), None),
    )
    out_specs = (
        P(("groups", "dp"), None),
        P("dp", "groups"),
        P(("groups", "dp"), None, None),
        P(("groups", "dp"), None, None),
    )
    return jax.shard_map(
        local_clustered if clustered else local, mesh=mesh, in_specs=in_specs, out_specs=out_specs, check_vma=False
    )
```

```python
import functools
import math

import jax
import jax.numpy as jnp
from jax import lax
from jax.experimental import pallas as pl
from jax.experimental.pallas import tpu as pltpu
from jax.sharding import PartitionSpec as P

HD = 128
KVH = 4
GROUP = 8
CHIPS = 4
SPAN = 16


adapter_scale = 2.0
neg_fill = -1e30


def build_mask(seg_ids, block_len):
    position = jnp.arange(seg_ids.shape[0])
    block_ids = position // block_len
    same_block = block_ids[:, None] == block_ids[None, :]
    same_seq = seg_ids[:, None] == seg_ids[None, :]
    causal = position[None, :] <= position[:, None]
    return same_block & same_seq & causal


def first_pass(query_tile, key_tile, grad_tile, keep_mask):
    tile_rows = query_tile.shape[0]
    query_heads = query_tile.reshape(tile_rows, KVH, GROUP, HD)
    key_heads = key_tile.reshape(tile_rows, KVH, HD)
    scores = jnp.einsum(
        "tkgd,skd->kgts", query_heads, key_heads, preferred_element_type=jnp.float32
    ) / math.sqrt(HD)
    scores = jnp.where(keep_mask[None, None], scores, neg_fill)
    attn_probs = jax.nn.softmax(scores, axis=-1)
    probs_b = attn_probs.astype(jnp.bfloat16)
    grad_heads = grad_tile.reshape(tile_rows, KVH, GROUP, HD)
    value_gradient = jnp.einsum(
        "kgts,tkgd->skd", probs_b, grad_heads, preferred_element_type=jnp.float32
    )
    return (attn_probs, probs_b, value_gradient.reshape(tile_rows, KVH * HD).astype(jnp.bfloat16))


def second_pass(attn_probs, probs_b, value_tile, key_tile, grad_tile):
    tile_rows = value_tile.shape[0]
    value_heads = value_tile.reshape(tile_rows, KVH, HD)
    key_heads = key_tile.reshape(tile_rows, KVH, HD)
    grad_heads = grad_tile.reshape(tile_rows, KVH, GROUP, HD)
    out_attn = jnp.einsum(
        "kgts,skd->tkgd", probs_b, value_heads, preferred_element_type=jnp.float32
    )
    dprobs = jnp.einsum(
        "tkgd,skd->kgts", grad_heads, value_heads, preferred_element_type=jnp.float32
    )
    row_delta = jnp.transpose(
        jnp.sum(grad_heads.astype(jnp.float32) * out_attn, axis=-1), (1, 2, 0)
    )[..., None]
    dscores = (attn_probs * (dprobs - row_delta)).astype(jnp.bfloat16)
    grad_heads_q = jnp.einsum(
        "kgts,skd->tkgd", dscores, key_heads, preferred_element_type=jnp.float32
    ) / math.sqrt(HD)
    return grad_heads_q.reshape(tile_rows, KVH * GROUP * HD).astype(jnp.bfloat16)


def local(
    x_rows,
    query_rows,
    key_rows,
    values_base,
    grad_out,
    adapt_down,
    adapt_up,
    block_tenant,
    owner_map,
    seq_ids,
):
    tok_rows = x_rows.shape[0]
    blk_count = block_tenant.shape[0]
    block_len = tok_rows // blk_count
    width = x_rows.shape[1]
    value_width = key_rows.shape[1]
    adapter_count = owner_map.shape[0]
    sliced_down, sliced_up = (
        lax.all_to_all(adapt_down, "dp", split_axis=1, concat_axis=0, tiled=True),
        lax.all_to_all(adapt_up, "dp", split_axis=1, concat_axis=0, tiled=True),
    )
    tenants = lax.all_gather(block_tenant, "dp", axis=0, tiled=True)
    lookup = tenants[:, None] == jnp.arange(adapter_count)[None, :]
    store_rows = jnp.sum(jnp.where(lookup, owner_map[None, :], 0), axis=1)
    picked_down = jnp.take(sliced_down, store_rows, axis=0)
    picked_up = jnp.take(sliced_up, store_rows, axis=0)
    my_down, tenant_up_weight = (
        lax.all_to_all(picked_down, "dp", split_axis=0, concat_axis=1, tiled=True),
        lax.all_to_all(picked_up, "dp", split_axis=0, concat_axis=1, tiled=True),
    )
    tile_rows = min(tok_rows, 512)
    tile_count = tok_rows // tile_rows
    query_tiles = query_rows.reshape(tile_count, tile_rows, -1)
    key_tiles = key_rows.reshape(tile_count, tile_rows, -1)
    grad_tiles = grad_out.reshape(tile_count, tile_rows, -1)
    seq_tiles = seq_ids.reshape(tile_count, tile_rows)
    keep_masks = jax.vmap(lambda ids: build_mask(ids, block_len))(seq_tiles)
    attn_probs, probs_b, value_gradient = jax.vmap(first_pass)(
        query_tiles, key_tiles, grad_tiles, keep_masks
    )
    dvalue_blocks = value_gradient.reshape(blk_count, block_len, value_width)
    x_blocks = x_rows.reshape(blk_count, block_len, width)
    hidden_rows = jnp.einsum(
        "btd,brd->btr", x_blocks, my_down, preferred_element_type=jnp.float32
    ).astype(jnp.bfloat16)
    adapter_values = jnp.einsum(
        "uzd,udv->uzv", hidden_rows, tenant_up_weight, preferred_element_type=jnp.float32
    )
    frozen_value_blocks = values_base.reshape(blk_count, block_len, value_width).astype(jnp.float32)
    value_rows = (frozen_value_blocks + adapter_scale * adapter_values).astype(jnp.bfloat16)
    hidden_gradient = (
        adapter_scale
        * jnp.einsum(
            "bte,bre->btr", dvalue_blocks, tenant_up_weight, preferred_element_type=jnp.float32
        )
    ).astype(jnp.bfloat16)
    part_down = jnp.einsum(
        "btr,btd->brd", hidden_gradient, x_blocks, preferred_element_type=jnp.float32
    )
    partial_up_weight = adapter_scale * jnp.einsum(
        "btr,bte->bre", hidden_rows, dvalue_blocks, preferred_element_type=jnp.float32
    )
    back_down, back_up = (
        lax.all_to_all(part_down, "dp", split_axis=1, concat_axis=0, tiled=True),
        lax.all_to_all(partial_up_weight, "dp", split_axis=1, concat_axis=0, tiled=True),
    )
    selector = (jnp.arange(adapter_count)[:, None] == store_rows[None, :]).astype(jnp.float32)
    sum_down = jnp.einsum("ab,brc->arc", selector, back_down, precision=lax.Precision.HIGHEST)
    sum_up = jnp.einsum("ab,brc->arc", selector, back_up, precision=lax.Precision.HIGHEST)
    grad_down, grad_up = (
        lax.all_to_all(
            sum_down.astype(jnp.bfloat16), "dp", split_axis=0, concat_axis=1, tiled=True
        ),
        lax.all_to_all(sum_up.astype(jnp.bfloat16), "dp", split_axis=0, concat_axis=1, tiled=True),
    )
    local_grad = jnp.einsum(
        "brd,btr->dbt", my_down, hidden_gradient, preferred_element_type=jnp.float32
    )
    local_grad = local_grad.reshape(width, tok_rows).astype(jnp.bfloat16)
    grad_input_t = lax.all_to_all(local_grad, "dp", split_axis=0, concat_axis=1, tiled=True)
    value_tiles = value_rows.reshape(tile_count, tile_rows, value_width)
    grad_query = jax.vmap(second_pass)(attn_probs, probs_b, value_tiles, key_tiles, grad_tiles)
    grad_query = grad_query.reshape(tok_rows, -1)
    return (grad_query, grad_input_t, grad_down, grad_up)


def cost(micros):
    return pl.CostEstimate(flops=0, bytes_accessed=int(micros * 3.3e4), transcendentals=0)


def eighth_of(device):
    return 4 * ((device >> 3) ^ (device & 1)) + ((device >> 1) & 3)


def run_copies(pairs, sems):
    copies = [pltpu.make_async_copy(src, dst, sems.at[k]) for k, (src, dst) in enumerate(pairs)]
    for copy in copies:
        copy.start()
    return copies


def columns(part, span):
    return pl.ds(pl.multiple_of(part * span, 128), span)


def pack_kernel(x_ref, down_ref, down_out, *refs):
    outs, (x_buf, down_buf, sems) = refs[: CHIPS - 1], refs[CHIPS - 1 :]
    me, group = lax.axis_index("dp"), lax.axis_index("groups")
    half, span = down_out.shape[1:]
    ranks = pl.ds(pl.multiple_of(group * half, 16), half)
    pairs = []
    for k in range(CHIPS - 1):
        chip = ((me >> 1) & 3) ^ (k + 1)
        for side in range(2):
            part = 4 * ((me >> 3) ^ side) + chip
            pairs.append((x_ref.at[:, columns(part, span)], x_buf.at[k, :, pl.ds(side * span, span)]))
    pairs.append((down_ref.at[0, ranks, :], down_buf))
    loads = run_copies(pairs, sems)
    pairs = [(x_buf.at[k], outs[k]) for k in range(CHIPS - 1)]
    for dest in range(SPAN):
        pairs.append((down_buf.at[:, pl.ds(eighth_of(dest) * span, span)], down_out.at[dest]))
    stores = [
        pltpu.make_async_copy(src, dst, sems.at[len(loads) + k])
        for k, (src, dst) in enumerate(pairs)
    ]
    for k in range(CHIPS - 1):
        loads[2 * k].wait()
        loads[2 * k + 1].wait()
        stores[k].start()
    loads[-1].wait()
    for copy in stores[CHIPS - 1 :]:
        copy.start()
    for copy in stores:
        copy.wait()


def store_kernel(tenant_ref, owner_ref, out_ref):
    for k in range(2):
        out_ref[k] = owner_ref[tenant_ref[k]]


def heads_in_rows(ref):
    return jnp.concatenate([ref[:, h * HD : (h + 1) * HD] for h in range(GROUP)], axis=0)


def probabilities(ids, keys, queries):
    length = ids.shape[1]
    across = jnp.broadcast_to(ids.astype(jnp.float32), (length, length))
    later = lax.broadcasted_iota(jnp.int32, (length, length), 1)
    earlier = lax.broadcasted_iota(jnp.int32, (length, length), 0)
    keep = (across == across.T) & (earlier <= later)
    scores = lax.dot_general(
        keys, queries, (((1,), (1,)), ((), ())), preferred_element_type=jnp.float32
    ) * (1.0 / math.sqrt(HD))
    scores = jnp.where(jnp.concatenate([keep] * GROUP, axis=1), scores, neg_fill)
    weights = jnp.exp(scores - jnp.max(scores, axis=0, keepdims=True))
    return weights * (1.0 / jnp.sum(weights, axis=0, keepdims=True))


def first_kernel(ids_ref, query_ref, key_ref, grad_ref, dval_ref):
    ids = ids_ref[pl.ds(pl.program_id(0), 1), :]
    probs = probabilities(ids, key_ref[...], heads_in_rows(query_ref)).astype(jnp.bfloat16)
    out = jnp.dot(probs, heads_in_rows(grad_ref), preferred_element_type=jnp.float32)
    dval_ref[...] = out.astype(jnp.bfloat16)


def second_kernel(ids_ref, query_ref, key_ref, value_ref, grad_ref, out_ref):
    ids = ids_ref[pl.ds(pl.program_id(0), 1), :]
    keys = key_ref[...]
    probs = probabilities(ids, keys, heads_in_rows(query_ref))
    dprobs = lax.dot_general(
        value_ref[...],
        heads_in_rows(grad_ref),
        (((1,), (1,)), ((), ())),
        preferred_element_type=jnp.float32,
    )
    rounded = probs.astype(jnp.bfloat16).astype(jnp.float32)
    delta = jnp.sum(rounded * dprobs, axis=0, keepdims=True)
    dscores = (probs * (dprobs - delta)).astype(jnp.bfloat16)
    turned = keys.astype(jnp.float32).T.astype(jnp.bfloat16)
    out = jnp.dot(turned, dscores, preferred_element_type=jnp.float32) * (1.0 / math.sqrt(HD))
    for head in range(GROUP):
        lanes = slice(head * HD, (head + 1) * HD)
        out_ref[:, lanes] = out[:, lanes].T.astype(jnp.bfloat16)


def grad_hidden_kernel(slot_ref, store_ref, dval_ref, up_ref, out_ref):
    rank = up_ref.shape[1]
    out = lax.dot_general(
        up_ref[0], dval_ref[...], (((1,), (1,)), ((), ())), preferred_element_type=jnp.float32
    )
    out_ref[pl.ds(0, rank), :] = (adapter_scale * out).astype(jnp.bfloat16)
    store = store_ref[pl.program_id(0)].astype(jnp.float32)
    below = jnp.full((16, out_ref.shape[1]), store, jnp.float32)
    out_ref[pl.ds(rank, 16), :] = below.astype(jnp.bfloat16)


def read_stores(values, rank, wide, stores, sem):
    for k, value in enumerate(values):
        row = value[pl.ds(rank, 16), :].astype(jnp.float32)[0:1, :]
        wide[pl.ds(k, 1), :] = row.astype(jnp.int32)
    copy = pltpu.make_async_copy(wide, stores, sem)
    copy.start()
    copy.wait()


def x_copies(x_ref, near, rows):
    me = lax.axis_index("dp")
    chip = (me >> 1) & 3
    span = rows.shape[2] // 2
    pairs = []
    for side in range(2):
        part = 4 * ((me >> 3) ^ side) + chip
        pairs.append((x_ref.at[:, columns(part, span)], rows.at[0, :, pl.ds(side * span, span)]))
    for k, ref in enumerate(near):
        pairs.append((ref, rows.at[k + 1]))
    return pairs


def hidden_kernel(x_ref, *refs):
    grads, near, downs, outs = refs[:4], refs[4:7], refs[7:11], refs[11:15]
    rows, down, wide, stores, sems = refs[15:]
    me, group = lax.axis_index("dp"), lax.axis_index("groups")
    core = me & 1
    span, half = downs[0].shape[2], downs[0].shape[1]
    block = x_ref.shape[0] // 2
    copies = run_copies(x_copies(x_ref, near, rows), sems)
    read_stores(grads, 2 * half, wide, stores, sems.at[len(copies)])
    for slot in range(CHIPS):
        for k in range(2):
            store = stores[slot, k * block]
            for kind, ref in enumerate(downs):
                ranks = pl.ds(pl.multiple_of((group ^ (kind & 1)) * half, 16), half)
                lanes = columns(core ^ (kind >> 1), span)
                copy = pltpu.make_async_copy(
                    ref.at[store], down.at[2 * slot + k, ranks, lanes], sems.at[len(copies) + 1]
                )
                copy.start()
                copies.append(copy)
    for copy in copies:
        copy.wait()
    for slot in range(CHIPS):
        for k in range(2):
            out = lax.dot_general(
                down[2 * slot + k],
                rows[slot, pl.ds(k * block, block), :],
                (((1,), (1,)), ((), ())),
                preferred_element_type=jnp.float32,
            )
            outs[slot][:, pl.ds(k * block, block)] = out


def grad_down_kernel(x_ref, *refs):
    grads, near, (keep_ref, send_ref, rows, total, wide, stores, sems) = refs[:4], refs[4:7], refs[7:]
    core = lax.axis_index("dp") & 1
    rank, span = keep_ref.shape[1:]
    block = x_ref.shape[0] // 2
    copies = run_copies(x_copies(x_ref, near, rows), sems)
    read_stores(grads, rank, wide, stores, sems.at[len(copies)])
    total[...] = jnp.zeros_like(total)
    for copy in copies:
        copy.wait()
    for slot in range(CHIPS):
        for k in range(2):
            total[stores[slot, k * block]] += jnp.dot(
                grads[slot][pl.ds(0, rank), pl.ds(k * block, block)],
                rows[slot, pl.ds(k * block, block), :],
                preferred_element_type=jnp.float32,
            )
    keep_ref[...] = total[:, :, columns(core, span)].astype(jnp.bfloat16)
    send_ref[...] = total[:, :, columns(1 - core, span)].astype(jnp.bfloat16)


def sum_kernel(part_ref, out_ref, token_ref):
    span = part_ref.shape[2]
    token_ref[...] = jnp.zeros_like(token_ref)
    for part in range(2 * CHIPS):
        one, two = [i for i in range(SPAN) if eighth_of(i) == part]
        out = part_ref[one].astype(jnp.float32) + part_ref[two].astype(jnp.float32)
        out_ref[0, :, pl.ds(part * span, span)] = out.astype(jnp.bfloat16)


def values_kernel(up_slot_ref, base_ref, dval_ref, up_ref, *refs):
    hidden_refs, (val_ref, term_ref) = refs[:CHIPS], refs[CHIPS + 1 :]
    block = base_ref.shape[0] // 2
    hidden = hidden_refs[0][...]
    for ref in hidden_refs[1:]:
        hidden = hidden + ref[...]
    hidden = hidden.astype(jnp.bfloat16)
    for k in range(2):
        rows = pl.ds(k * block, block)
        part = hidden[:, k * block : (k + 1) * block]
        added = lax.dot_general(
            part,
            up_ref[up_slot_ref[k]],
            (((0,), (0,)), ((), ())),
            preferred_element_type=jnp.float32,
        )
        val_ref[rows, :] = (base_ref[rows, :].astype(jnp.float32) + adapter_scale * added).astype(
            jnp.bfloat16
        )
        term = jnp.dot(part, dval_ref[rows, :], preferred_element_type=jnp.float32)
        term_ref[k] = (adapter_scale * term).astype(jnp.bfloat16)


def place_kernel(slot_ref, own_ref, came_ref, keep_ref, send_ref):
    keep_ref[...] = jnp.zeros_like(keep_ref)
    send_ref[...] = jnp.zeros_like(send_ref)
    for k in range(4):
        slot = slot_ref[k]
        term = (own_ref, came_ref)[k // 2][k % 2].astype(jnp.float32)
        for side, ref in enumerate((keep_ref, send_ref)):

            @pl.when((slot & 3) == 2 * side)
            def _():
                place = ref.at[slot >> 2]
                place[...] = (place[...].astype(jnp.float32) + term).astype(ref.dtype)


def halve_kernel(kept_ref, came_ref, *outs, extra=0):
    outs = outs[extra:]
    for k in range(kept_ref.shape[0]):
        ref = outs[k % len(outs)]
        ref[k // len(outs)] = (kept_ref[k] + came_ref[k].astype(jnp.float32)).astype(ref.dtype)


def grad_input_kernel(grad_ref, *refs):
    downs, (out_ref, down, wide, turned, marks, stores, sems) = refs[:4], refs[4:]
    me, group = lax.axis_index("dp"), lax.axis_index("groups")
    core = me & 1
    block = grad_ref.shape[2] // 2
    feats, span = out_ref.shape[0], down.shape[2]
    half = down.shape[1] // 2
    window = wide.shape[0]

    def places(kind):
        ranks = pl.ds(pl.multiple_of((group ^ kind) * half, 16), half)
        return down.at[:, ranks, :]

    for side in range(2):

        @pl.when(core == side)
        def _():
            for kind in range(2):
                src = downs[2 * side + kind]
                pltpu.make_async_copy(src, places(kind), sems.at[kind]).start()

    read_stores([grad_ref.at[k] for k in range(SPAN)], 2 * half, marks, stores, sems.at[2])
    for kind in range(2):
        pltpu.make_async_copy(downs[kind], places(kind), sems.at[kind]).wait()
    lanes = pl.ds(pl.multiple_of(core * (span - window), 128), window)
    skip = pl.ds(pl.multiple_of(core * (window - feats), 16), feats)
    for store in range(SPAN):
        wide[...] = down[store, :, lanes].astype(jnp.float32).T
        turned[store] = wide[skip, :].astype(jnp.bfloat16)
    for mask in range(SPAN):
        for k in range(2):
            out = jnp.dot(
                turned[stores[mask, k * block]],
                grad_ref[mask, pl.ds(0, 2 * half), pl.ds(k * block, block)],
                preferred_element_type=jnp.float32,
            )
            at = pl.multiple_of(((mask ^ me) * 2 + k) * block, 128)
            out_ref[:, pl.ds(at, block)] = out.astype(jnp.bfloat16)


def together(*values):
    return lax.optimization_barrier(values)


def swap(value, mask):
    return lax.ppermute(value, "dp", [(i, i ^ mask) for i in range(SPAN)])


def spread(value, masks, done=()):
    for mask in masks:
        axis = sum(other > mask for other in done)
        value = jnp.stack([value, swap(value, mask)], axis=axis)
        done = done + (mask,)
    return value


def local_clustered(
    x_rows,
    query_rows,
    key_rows,
    values_base,
    grad_out,
    adapt_down,
    adapt_up,
    block_tenant,
    owner_map,
    seq_ids,
):
    tok_rows, width = x_rows.shape
    value_width = key_rows.shape[1]
    query_width = query_rows.shape[1]
    rank = adapt_down.shape[1]
    blocks, block = seq_ids.shape
    heads = value_width // HD
    span = width // (2 * CHIPS)
    group_width = GROUP * HD
    bf16, f32 = jnp.bfloat16, jnp.float32
    any_spec = pl.BlockSpec(memory_space=pltpu.HBM)
    smem_spec = pl.BlockSpec(memory_space=pltpu.SMEM)
    vmem_spec = pl.BlockSpec(memory_space=pltpu.VMEM)
    shape = jax.ShapeDtypeStruct
    params = pltpu.CompilerParams(vmem_limit_bytes=16 * 1024 * 1024)
    big = pltpu.CompilerParams(vmem_limit_bytes=60 * 1024 * 1024)
    wide_spec = pl.BlockSpec((block, group_width), lambda b, h: (b, h))
    head_spec = pl.BlockSpec((block, HD), lambda b, h: (b, h))

    down_pack, *x_packs = pl.pallas_call(
        pack_kernel,
        in_specs=[any_spec] * 2,
        out_specs=[any_spec] * CHIPS,
        out_shape=[shape((SPAN, rank // 2, span), bf16)]
        + [shape((tok_rows, 2 * span), bf16)] * (CHIPS - 1),
        scratch_shapes=[
            pltpu.VMEM((CHIPS - 1, tok_rows, 2 * span), bf16),
            pltpu.VMEM((rank // 2, width), bf16),
            pltpu.SemaphoreType.DMA((SPAN + 3 * CHIPS,)),
        ],
        compiler_params=big,
        cost_estimate=cost(2.5),
        name="pack",
    )(x_rows, adapt_down)

    own_stores = pl.pallas_call(
        store_kernel,
        in_specs=[smem_spec] * 2,
        out_specs=smem_spec,
        out_shape=shape((blocks,), jnp.int32),
        name="store_rows",
    )(block_tenant, owner_map)

    dvalues = pl.pallas_call(
        first_kernel,
        grid=(blocks, heads),
        in_specs=[vmem_spec, wide_spec, head_spec, wide_spec],
        out_specs=head_spec,
        out_shape=shape((tok_rows, value_width), bf16),
        compiler_params=params,
        cost_estimate=cost(7),
        name="first_pass",
    )(seq_ids, query_rows, key_rows, grad_out)

    up_pair = jnp.concatenate([adapt_up, swap(adapt_up, 8)])
    x_packs[0], x_packs[1], x_packs[2], up_pair = together(*x_packs, up_pair)
    peers = [[first + 2 * k for k in range(CHIPS)] for first in (0, 1, 8, 9)]
    near_up = lax.all_to_all(
        jnp.broadcast_to(up_pair, (CHIPS,) + up_pair.shape), "dp", 0, 0, axis_index_groups=peers
    )
    near = [swap(x_packs[k], 2 * (k + 1)) for k in range(CHIPS - 1)]
    down_pack, near_up = together(down_pack, near_up)
    down_own = lax.all_to_all(down_pack, "dp", split_axis=0, concat_axis=0, tiled=True)
    near[0], near[1], near_up, dvalues = together(near[0], near[1], near_up, dvalues)
    all_up = jnp.stack([near_up, swap(near_up, 1)]).reshape((SPAN,) + adapt_up.shape[1:])
    me = lax.axis_index("dp")
    chip_slots = jnp.concatenate([own_stores, swap(own_stores, 1)]) ^ me
    slots = own_stores ^ me
    up_slots = 8 * (slots & 1) + (own_stores & 6) + (slots >> 3)

    hidden_gradient = pl.pallas_call(
        grad_hidden_kernel,
        grid_spec=pltpu.PrefetchScalarGridSpec(
            num_scalar_prefetch=2,
            grid=(blocks,),
            in_specs=[
                pl.BlockSpec((block, value_width), lambda b, slot, store: (b, 0)),
                pl.BlockSpec((1, rank, value_width), lambda b, slot, store: (slot[b], 0, 0)),
            ],
            out_specs=pl.BlockSpec((rank + 16, block), lambda b, slot, store: (0, b)),
        ),
        out_shape=shape((rank + 16, tok_rows), bf16),
        compiler_params=params,
        cost_estimate=cost(1),
        name="grad_hidden",
    )(up_slots, own_stores, dvalues, all_up)
    down_own, hidden_gradient = together(down_own, hidden_gradient)
    near_grad = [hidden_gradient] + [swap(hidden_gradient, 2 * k) for k in range(1, CHIPS)]
    down_other = lax.ppermute(down_own, "groups", [(0, 1), (1, 0)])
    down_other, *held = together(down_other, near[2], *near_grad)
    downs = [down_own, down_other, swap(down_own, 1), swap(down_other, 1)]

    hidden_parts = pl.pallas_call(
        hidden_kernel,
        in_specs=[any_spec] + [vmem_spec] * CHIPS + [any_spec] * (CHIPS + 3),
        out_specs=[vmem_spec] * CHIPS,
        out_shape=[shape((rank, tok_rows), f32)] * CHIPS,
        scratch_shapes=[
            pltpu.VMEM((CHIPS, tok_rows, 2 * span), bf16),
            pltpu.VMEM((2 * CHIPS, rank, 2 * span), bf16),
            pltpu.VMEM((8, tok_rows), jnp.int32),
            pltpu.SMEM((8, tok_rows), jnp.int32),
            pltpu.SemaphoreType.DMA((9 * CHIPS + 2,)),
        ],
        compiler_params=params,
        cost_estimate=cost(3),
        name="hidden",
    )(x_rows, *held[1:], near[0], near[1], held[0], *downs)
    own_part = hidden_parts[0]
    hidden_parts = [swap(hidden_parts[k], 2 * k) for k in range(1, CHIPS)]

    down_keep, down_send = pl.pallas_call(
        grad_down_kernel,
        in_specs=[any_spec] + [vmem_spec] * CHIPS + [any_spec] * (CHIPS - 1),
        out_specs=[vmem_spec] * 2,
        out_shape=[shape((SPAN, rank, span), bf16)] * 2,
        scratch_shapes=[
            pltpu.VMEM((CHIPS, tok_rows, 2 * span), bf16),
            pltpu.VMEM((SPAN, rank, 2 * span), f32),
            pltpu.VMEM((8, tok_rows), jnp.int32),
            pltpu.SMEM((8, tok_rows), jnp.int32),
            pltpu.SemaphoreType.DMA((CHIPS + 2,)),
        ],
        compiler_params=params,
        cost_estimate=cost(3),
        name="grad_down",
    )(x_rows, *near_grad, *near)
    all_grad = jnp.stack(near_grad)
    far_grad, *hidden_parts = together(swap(all_grad, 8), *hidden_parts)
    down_parts = (down_keep.astype(f32) + swap(down_send, 1).astype(f32)).astype(bf16)
    value_rows, terms = pl.pallas_call(
        values_kernel,
        in_specs=[smem_spec] + [vmem_spec] * (3 + CHIPS) + [any_spec],
        out_specs=[vmem_spec] * 2,
        out_shape=[
            shape((tok_rows, value_width), bf16),
            shape((blocks, rank, value_width), bf16),
        ],
        compiler_params=params,
        cost_estimate=cost(1),
        name="values",
    )(up_slots, values_base, dvalues, all_up, own_part, *hidden_parts, down_parts)

    down_parts, terms, far_grad = together(down_parts, terms, far_grad)
    all_grad = jnp.stack([all_grad, far_grad])
    all_grad = jnp.stack([all_grad, swap(all_grad, 1)], axis=2)
    all_grad = all_grad.reshape((SPAN,) + hidden_gradient.shape)
    down_parts = lax.all_to_all(down_parts, "dp", split_axis=0, concat_axis=0, tiled=True)


    grad_query = pl.pallas_call(
        second_kernel,
        grid=(blocks, heads),
        in_specs=[vmem_spec, wide_spec, head_spec, head_spec, wide_spec],
        out_specs=wide_spec,
        out_shape=shape((tok_rows, query_width), bf16),
        compiler_params=params,
        cost_estimate=cost(9),
        name="second_pass",
    )(seq_ids, query_rows, key_rows, value_rows, grad_out)

    feats = width // SPAN
    window = -(-feats // 128) * 128
    grad_input_t = pl.pallas_call(
        grad_input_kernel,
        in_specs=[vmem_spec] + [any_spec] * 4,
        out_specs=vmem_spec,
        out_shape=shape((feats, SPAN * tok_rows), bf16),
        scratch_shapes=[
            pltpu.VMEM((SPAN, rank, span), bf16),
            pltpu.VMEM((window, rank), f32),
            pltpu.VMEM((SPAN, feats, rank), bf16),
            pltpu.VMEM((SPAN, tok_rows), jnp.int32),
            pltpu.SMEM((SPAN, tok_rows), jnp.int32),
            pltpu.SemaphoreType.DMA((3,)),
        ],
        compiler_params=params,
        cost_estimate=cost(7),
        name="grad_input",
    )(all_grad, *downs)

    grad_down, token = pl.pallas_call(
        sum_kernel,
        in_specs=[vmem_spec],
        out_specs=[vmem_spec] * 2,
        out_shape=[shape((1, rank, width), bf16), shape((8, 128), f32)],
        compiler_params=params,
        cost_estimate=cost(2),
        name="sum_down",
    )(down_parts)
    kept, sent = pl.pallas_call(
        place_kernel,
        in_specs=[smem_spec] + [vmem_spec] * 2,
        out_specs=[vmem_spec] * 2,
        out_shape=[
            shape((SPAN // 4, rank, value_width), f32),
            shape((SPAN // 4, rank, value_width), bf16),
        ],
        compiler_params=params,
        cost_estimate=cost(1),
        name="place",
    )(chip_slots, terms, swap(terms, 1))
    for mask in (2, 4, 8):
        if mask == 4:
            sent, grad_query = together(sent, grad_query)
        if mask == 8:
            sent, grad_input_t = together(sent, grad_input_t)
        came = swap(sent, mask)
        last = (token,) if mask == 8 else ()
        count = max(came.shape[0] // 2, 1)
        outs = [shape((count,) + came.shape[1:], bf16)]
        if mask < 8:
            outs = [shape(outs[0].shape, f32)] + outs
        halves = pl.pallas_call(
            functools.partial(halve_kernel, extra=len(last)),
            in_specs=[vmem_spec] * 2 + [any_spec] * len(last),
            out_specs=[vmem_spec] * len(outs),
            out_shape=outs,
            compiler_params=params,
            cost_estimate=cost(1),
            name="halve",
        )(kept, came, *last)
        kept, sent = halves[0], halves[-1]
    grad_up = sent

    return (grad_query, grad_input_t, grad_down, grad_up)


def solution(mesh):
    clustered = mesh.shape["dp"] == SPAN and mesh.shape["groups"] == 2
    in_specs = (
        P(("groups", "dp"), None),
        P(("groups", "dp"), None),
        P(("groups", "dp"), None),
        P(("groups", "dp"), None),
        P(("groups", "dp"), None),
        P("dp", None, None),
        P("dp", None, None),
        P(("groups", "dp")),
        P(),
        P(("groups", "dp"), None),
    )
    out_specs = (
        P(("groups", "dp"), None),
        P("dp", "groups"),
        P(("groups", "dp"), None, None),
        P(("groups", "dp"), None, None),
    )
    return jax.shard_map(
        local_clustered if clustered else local, mesh=mesh, in_specs=in_specs, out_specs=out_specs, check_vma=False
    )
```
